32 devices in a mesh: seq: 2 (over y), fsdp: 16 (over z, x, core).
Axes of the slice: x: 2, y: 2, z: 4, core: 2. Of those that a mesh axis runs over, the one named last changes fastest.
Arguments:
- tokens: bfloat16 [8192, 2048], P(('fsdp', 'seq')), may hold values from -6 to 6
- attn_gain: bfloat16 [2048], P(('seq', 'fsdp')), may hold values from 0.5 to 1.5
- w_query: bfloat16 [2048, 1024], P(('seq', 'fsdp')), may hold values from -0.125 to 0.125
- w_key: bfloat16 [2048, 1024], P(('seq', 'fsdp')), may hold values from -0.125 to 0.125
- w_value: bfloat16 [2048, 2048], P(('seq', 'fsdp')), may hold values from -0.125 to 0.125
- w_down_rank: bfloat16 [2048, 16], P(('seq', 'fsdp')), may hold values from -0.125 to 0.125
- w_up_rank: bfloat16 [16, 1024], P(None, ('seq', 'fsdp')), may hold values from -1.5 to 1.5
- gate_bias: bfloat16 [1024], P(('seq', 'fsdp')), may hold values from -1 to 11
- w_outgate: bfloat16 [2048, 2048], P(('seq', 'fsdp')), may hold values from -0.125 to 0.125
- head_gain: bfloat16 [512], P(('seq', 'fsdp')), may hold values from 0.5 to 1.5
- w_output: bfloat16 [2048, 2048], P(('seq', 'fsdp')), may hold values from -0.25 to 0.25
- ffn_gain: bfloat16 [2048], P(('seq', 'fsdp')), may hold values from 0.5 to 1.5
- w_gate: bfloat16 [2048, 5632], P(('seq', 'fsdp')), may hold values from -0.125 to 0.125
- w_up: bfloat16 [2048, 5632], P(('seq', 'fsdp')), may hold values from -0.125 to 0.125
- w_down: bfloat16 [5632, 2048], P(('seq', 'fsdp')), may hold values from -0.15625 to 0.15625
- doc_starts: int32 [32], P('fsdp'), may hold values from 0 to 256, as said below
- cotangent: bfloat16 [8192, 2048], P(('fsdp', 'seq')), may hold values from -6 to 6
Outputs:
- layer_output: bfloat16 [8192, 2048], P(('fsdp', 'seq'))
- input_grad: bfloat16 [8192, 2048], P(('fsdp', 'seq'))
- attn_gain_grad: float32 [2048], P(('seq', 'fsdp'))
- w_query_grad: float32 [2048, 1024], P(('seq', 'fsdp'))
- w_key_grad: float32 [2048, 1024], P(('seq', 'fsdp'))
- w_value_grad: float32 [2048, 2048], P(('seq', 'fsdp'))
- w_down_rank_grad: float32 [2048, 16], P(('seq', 'fsdp'))
- w_up_rank_grad: float32 [16, 1024], P(None, ('seq', 'fsdp'))
- gate_bias_grad: float32 [1024], P(('seq', 'fsdp'))
- w_outgate_grad: float32 [2048, 2048], P(('seq', 'fsdp'))
- head_gain_grad: float32 [512], P(('seq', 'fsdp'))
- w_output_grad: float32 [2048, 2048], P(('seq', 'fsdp'))
- ffn_gain_grad: float32 [2048], P(('seq', 'fsdp'))
- w_gate_grad: float32 [2048, 5632], P(('seq', 'fsdp'))
- w_up_grad: float32 [2048, 5632], P(('seq', 'fsdp'))
- w_down_grad: float32 [5632, 2048], P(('seq', 'fsdp'))
The draws below stay inside these ranges and needn't reach their ends.
Inputs may be any that keep to these rules, and one draw needn't show every extreme that they name: `doc_starts`: segment 0 holds a document start after its first token, segment 32 - 1 holds one, no other segment holds one.
All inputs are finite; a program needn't handle non-finite values.
Results may differ from the reference program's by a relative error of at most 0.025.
The reference program's roundings to bfloat16 on the way count: a program that leaves them out, or rounds other values in their place, can miss the bound.
Values may be sent and summed in bfloat16 or wider, within the bound.
No kernel may reach another device: no remote copies, remote signals or barrier semaphores. Data moves between devices by JAX's collectives and lax.ppermute only.
A program may use at most 448 MiB of HBM per device.

```python
from functools import partial
import jax
import jax.numpy as jnp
from jax import lax

D = 2048
H = 4
DK = 1024
DV = 2048
RANK = 16
FF = 5632
SPAN = 64
TOK_DEV = 256
HK = 256
HV = 512
SEGS = 32
TOKENS = 8192


def draw_gate_bias(key, part):
    key = jax.random.fold_in(key, 7)
    pick_key, slow_key, fast_key = jax.random.split(key, 3)
    slow_rows = jax.random.bernoulli(pick_key, 0.5, (DK,))
    slow_values = jax.random.uniform(slow_key, (DK,), jnp.float32, 8.0, 11.0)
    fast_values = jax.random.uniform(fast_key, (DK,), jnp.float32, -1.0, 4.0)
    return jnp.where(slow_rows, slow_values, fast_values).astype(jnp.bfloat16)


def draw_doc_starts(key, part):
    key = jax.random.fold_in(key, 13)
    first_key, last_key = jax.random.split(key)
    first_start = jax.random.randint(first_key, (), 1, TOK_DEV)
    last_start = jax.random.randint(last_key, (), 0, TOK_DEV)
    segment = jnp.arange(SEGS, dtype=jnp.int32)
    return jnp.where(segment == 0, first_start, jnp.where(segment == SEGS - 1, last_start, TOK_DEV)).astype(jnp.int32)


def shard_levels(key, dims, shards, least, largest):
    loudness, own = 1.0, jax.random.fold_in(key, 6)
    for axis_at, shards_of in shards:
        steps = jnp.exp(jax.random.uniform(jax.random.fold_in(own, axis_at), (shards_of,), jnp.float32, least / len(shards), largest / len(shards)))
        loudness = loudness * jnp.repeat(steps, dims[axis_at] // shards_of).reshape([-1 if axis == axis_at else 1 for axis in range(len(dims))])
    return loudness


def bell_draw(own_key, dims, spread, bound, cuts=(), kind=jnp.bfloat16):
    result = spread * jax.random.normal(own_key, dims, jnp.float32)
    if cuts:
        result = result * shard_levels(own_key, dims, cuts, -0.22, 0.18)
    return jnp.clip(result, -bound, bound).astype(kind)


def setup_inputs(seed: int = 0) -> dict:
    key_of = jax.random.split(jax.random.key(seed), 18)
    tokens = bell_draw(key_of[0], (TOKENS, D), 1.0, 6.0, ((0, 32),))
    attn_gain = jnp.clip(1.0 + 0.1 * jax.random.normal(key_of[1], (D,), jnp.float32), 0.5, 1.5).astype(jnp.bfloat16)
    w_query = bell_draw(key_of[2], (D, DK), D ** -0.5, 0.125, ((0, 32),))
    w_key = bell_draw(key_of[3], (D, DK), D ** -0.5, 0.125, ((0, 32),))
    w_value = bell_draw(key_of[4], (D, DV), D ** -0.5, 0.125, ((0, 32),))
    w_down_rank = bell_draw(key_of[5], (D, RANK), D ** -0.5, 0.125, ((0, 32),))
    w_up_rank = bell_draw(key_of[6], (RANK, DK), RANK ** -0.5, 1.5, ((1, 32),))
    gate_bias = draw_gate_bias(jax.random.fold_in(key_of[17], 71), 0)
    w_outgate = bell_draw(key_of[8], (D, DV), D ** -0.5, 0.125, ((0, 32),))
    head_gain = jnp.clip(1.0 + 0.1 * jax.random.normal(key_of[9], (HV,), jnp.float32), 0.5, 1.5).astype(jnp.bfloat16)
    w_output = bell_draw(key_of[10], (DV, D), (DV // 4) ** -0.5, 0.25, ((0, 32),))
    ffn_gain = jnp.clip(1.0 + 0.1 * jax.random.normal(key_of[11], (D,), jnp.float32), 0.5, 1.5).astype(jnp.bfloat16)
    w_gate = bell_draw(key_of[12], (D, FF), D ** -0.5, 0.125, ((0, 32),))
    w_up = bell_draw(key_of[13], (D, FF), D ** -0.5, 0.125, ((0, 32),))
    w_down = bell_draw(key_of[14], (FF, D), (FF // 4) ** -0.5, 0.15625, ((0, 32),))
    doc_starts = draw_doc_starts(jax.random.fold_in(key_of[17], 71), 0)
    cotangent = bell_draw(key_of[16], (TOKENS, D), 1.0, 6.0, ((0, 32),))
    return dict(tokens=tokens, attn_gain=attn_gain, w_query=w_query, w_key=w_key, w_value=w_value, w_down_rank=w_down_rank, w_up_rank=w_up_rank, gate_bias=gate_bias, w_outgate=w_outgate, head_gain=head_gain, w_output=w_output, ffn_gain=ffn_gain, w_gate=w_gate, w_up=w_up, w_down=w_down, doc_starts=doc_starts, cotangent=cotangent)


epsilon = 1e-06
gate_scale = 16.0

@jax.custom_vjp
def low(v):
    return lax.optimization_barrier(v.astype(jnp.bfloat16)).astype(jnp.float32)

@jax.custom_vjp
def low_back(v):
    return v

def low_keep(v):
    return (low(v), None)

def low_pass(kept, grad):
    return (grad,)

def back_keep(v):
    return (v, None)

def back_low(kept, grad):
    return (low(grad),)
low.defvjp(low_keep, low_pass)
low_back.defvjp(back_keep, back_low)

def exact_dot(left, right):
    return jnp.dot(left, right, precision=lax.Precision.HIGHEST)

def precise_einsum(form, left, right):
    return jnp.einsum(form, left, right, precision=lax.Precision.HIGHEST)

def norm_rows(value_rows, gain):
    return value_rows * lax.rsqrt(lax.optimization_barrier(jnp.mean(value_rows * value_rows, axis=-1, keepdims=True)) + epsilon) * gain

def head_norm(value_rows, gain):
    shaped = value_rows.reshape(value_rows.shape[0], -1, HV)
    scaled = shaped * lax.rsqrt(lax.optimization_barrier(jnp.mean(shaped * shaped, axis=-1, keepdims=True)) + epsilon) * gain
    return scaled.reshape(value_rows.shape)

def span_core(carried_state, pieces):
    queries, keys_in, value_rows, decays, starts_flag = pieces
    length = starts_flag.shape[0]
    causal = (lax.broadcasted_iota(jnp.int32, (length, length), 0) >= lax.broadcasted_iota(jnp.int32, (length, length), 1)).astype(starts_flag.dtype)
    running = precise_einsum('ts,hsk->htk', causal, decays)
    doc_count = exact_dot(causal, starts_flag)
    expanded_rows = queries * jnp.exp(running)
    shrunk = keys_in * jnp.exp(-running)
    score_matrix = precise_einsum('htk,hsk->hts', expanded_rows, shrunk)
    same_doc = (doc_count[:, None] == doc_count[None, :]) & (causal > 0)
    score_matrix = jnp.where(same_doc[None, :, :], score_matrix, 0.0)
    unfinished_rows = doc_count == 0.0
    output_rows = precise_einsum('xbe,xeg->xbg', score_matrix, value_rows) + jnp.where(unfinished_rows[None, :, None], precise_einsum('cze,cer->czr', expanded_rows, carried_state), 0.0)
    closing_sum = running[:, -1, :]
    tail_rows = doc_count == doc_count[-1]
    ending_flags = jnp.where(tail_rows[None, :, None], keys_in * jnp.exp(closing_sum[:, None, :] - running), 0.0)
    unbroken_mask = doc_count[-1] == 0.0
    next_carried_state = jnp.where(unbroken_mask, jnp.exp(closing_sum)[:, :, None] * carried_state, 0.0) + precise_einsum('deo,dew->dow', ending_flags, value_rows)
    return (next_carried_state, output_rows)

def mixer(queries, keys_in, value_rows, logits, starts_flag):
    spans = TOKENS // SPAN

    def to_blocks(array, width):
        return array.reshape(spans, SPAN, H, width).transpose(0, 2, 1, 3)
    decays = jax.nn.log_sigmoid(logits) / gate_scale
    initial = jnp.zeros((H, HK, HV), dtype=queries.dtype)
    pieces = (to_blocks(queries, HK) * HK ** (-0.5), to_blocks(keys_in, HK), to_blocks(value_rows, HV), to_blocks(decays, HK), starts_flag.reshape(spans, SPAN))
    final_carry, output_rows = lax.scan(jax.checkpoint(span_core), initial, pieces)
    return output_rows.transpose(0, 2, 1, 3).reshape(TOKENS, DV)

def forward(inputs, attn_gain, w_query, w_key, w_value, w_down_rank, w_up_rank, gate_bias, w_outgate, head_gain, w_output, ffn_gain, w_gate, w_up, w_down, starts_flag):
    normed_in = low(norm_rows(inputs, attn_gain))
    queries = low(low_back(exact_dot(normed_in, w_query)))
    keys_in = low(low_back(exact_dot(normed_in, w_key)))
    value_rows = low(low_back(exact_dot(normed_in, w_value)))
    rank_low = low(low_back(exact_dot(normed_in, w_down_rank)))
    logits = low(low_back(exact_dot(rank_low, w_up_rank) + gate_bias))
    outgate = low_back(exact_dot(normed_in, w_outgate))
    mixed_tokens = low(low_back(mixer(queries, keys_in, value_rows, logits, starts_flag)))
    gated = low(head_norm(mixed_tokens, head_gain) * jax.nn.silu(outgate))
    resid = inputs + low_back(exact_dot(gated, w_output))
    normed_mid = low(norm_rows(resid, ffn_gain))
    gate_pre = low_back(exact_dot(normed_mid, w_gate))
    up_pre = low_back(exact_dot(normed_mid, w_up))
    hidden = low(jax.nn.silu(gate_pre) * up_pre)
    return resid + exact_dot(hidden, w_down)

def reference(tokens, attn_gain, w_query, w_key, w_value, w_down_rank, w_up_rank, gate_bias, w_outgate, head_gain, w_output, ffn_gain, w_gate, w_up, w_down, doc_starts, cotangent):
    starts_flag = (jnp.arange(TOK_DEV, dtype=jnp.int32)[None, :] == doc_starts[:, None].astype(jnp.int32)).astype(jnp.float32).reshape(TOKENS)
    output, pullback = jax.vjp(partial(forward, starts_flag=starts_flag), tokens.astype(jnp.float32), attn_gain.astype(jnp.float32), w_query.astype(jnp.float32), w_key.astype(jnp.float32), w_value.astype(jnp.float32), w_down_rank.astype(jnp.float32), w_up_rank.astype(jnp.float32), gate_bias.astype(jnp.float32), w_outgate.astype(jnp.float32), head_gain.astype(jnp.float32), w_output.astype(jnp.float32), ffn_gain.astype(jnp.float32), w_gate.astype(jnp.float32), w_up.astype(jnp.float32), w_down.astype(jnp.float32))
    grads = pullback(cotangent.astype(jnp.float32))
    return (output.astype(jnp.bfloat16), grads[0].astype(jnp.bfloat16), grads[1], grads[2], grads[3], grads[4], grads[5], grads[6], grads[7], grads[8], grads[9], grads[10], grads[11], grads[12], grads[13], grads[14])
```

```python
import jax
import jax.numpy as jnp
from jax import lax
from jax.sharding import PartitionSpec as P

SPAN = 64
HK = 256
HV = 512
HEADS = 4
EPS = 1e-06
GATE_SCALE = 16.0
BOTH = ("seq", "fsdp")
F32 = jnp.float32
BF16 = jnp.bfloat16


def dot(left, right):
    return jnp.dot(left, right, preferred_element_type=F32)


def dot_rows(left, right):
    return lax.dot_general(left, right, (((0,), (0,)), ((), ())), preferred_element_type=F32)


def dot_cols(left, right):
    return lax.dot_general(left, right, (((1,), (1,)), ((), ())), preferred_element_type=F32)


def ein(form, left, right):
    return jnp.einsum(form, left, right, preferred_element_type=F32)


class Place:
    def __init__(self):
        self.fsdp = lax.axis_size("fsdp")
        self.line_size = self.fsdp // 4
        index = lax.axis_index("fsdp")
        self.seq = lax.axis_index("seq")
        self.core = index % 2
        self.side = (index // 2) % 2
        self.line = index // 4
        self.groups = [
            [4 * a + 2 * b + c for a in range(self.line_size) for c in range(2)] for b in range(2)
        ]

    def send(self, value, move):
        pairs = []
        for s in range(2):
            for a in range(self.line_size):
                for b in range(2):
                    for c in range(2):
                        to = move(s, a, b, c)
                        if 0 <= to[1] < self.line_size:
                            source = s * self.fsdp + 4 * a + 2 * b + c
                            target = to[0] * self.fsdp + 4 * to[1] + 2 * to[2] + to[3]
                            pairs.append((source, target))
        return lax.ppermute(value, BOTH, pairs)

    def over_side(self, value):
        return self.send(value, lambda s, a, b, c: (s, a, 1 - b, c))

    def over_seq(self, value):
        return self.send(value, lambda s, a, b, c: (1 - s, a, b, c))

    def over_both(self, value):
        return self.send(value, lambda s, a, b, c: (1 - s, a, 1 - b, c))

    def over_core(self, value):
        return self.send(value, lambda s, a, b, c: (s, a, b, 1 - c))

    def along(self, value, step):
        return self.send(value, lambda s, a, b, c: (s, a + step, b, c))

    def swap_top(self, value):
        half = self.line_size // 2
        return self.send(value, lambda s, a, b, c: (s, b * half + a % half, a // half, c))


def pair(which, own, other):
    first = which == 0
    return jnp.stack([jnp.where(first, own, other), jnp.where(first, other, own)])


def exchange_quarters(here, blocks):
    me = 2 * here.seq + here.side
    take = lambda i: lax.dynamic_index_in_dim(blocks, i, 0, keepdims=False)
    own = take(me)
    side = here.over_side(take(me ^ 1))
    seq = here.over_seq(take(me ^ 2))
    both = here.over_both(take(me ^ 3))
    rows = pair(here.seq, pair(here.side, own, side), pair(here.side, seq, both))
    return rows.reshape((4,) + own.shape)


def gather_tokens(here, rows):
    half = rows.shape[0] // 2
    top, low = rows[:half], rows[half:]
    top_side = here.over_side(top)
    low_seq = here.over_seq(low)
    top_pair = jnp.stack([top, top_side])
    low_pair = jnp.stack([low, low_seq])
    top_far = here.over_seq(top_pair)
    low_far = here.over_side(low_pair)
    own = jnp.concatenate([top, low])
    side = jnp.concatenate([top_side, low_far[0]])
    seq = jnp.concatenate([top_far[0], low_seq])
    both = jnp.concatenate([top_far[1], low_far[1]])
    out = pair(here.side, pair(here.seq, own, seq), pair(here.seq, side, both))
    return out.reshape((4 * rows.shape[0],) + rows.shape[1:])


def scatter_tokens(here, rows):
    tok, width = rows.shape[0] // 4, rows.shape[1]
    half = tok // 2
    blocks = rows.reshape(2, 2, 2, half, width)
    top, low = blocks[:, :, 0], blocks[:, :, 1]
    pick = lambda a, i, axis: lax.dynamic_index_in_dim(a, i, axis, keepdims=False)
    top_in = here.over_side(pick(top, 1 - here.side, 0))
    low_in = here.over_seq(pick(low, 1 - here.seq, 1))
    top_sum = pick(top, here.side, 0).astype(F32) + top_in.astype(F32)
    low_sum = pick(low, here.seq, 1).astype(F32) + low_in.astype(F32)
    top_far = here.over_seq(pick(top_sum, 1 - here.seq, 0).astype(BF16))
    low_far = here.over_side(pick(low_sum, 1 - here.side, 0).astype(BF16))
    return jnp.concatenate(
        [
            pick(top_sum, here.seq, 0) + top_far.astype(F32),
            pick(low_sum, here.side, 0) + low_far.astype(F32),
        ]
    )


def gather_line(here, rows):
    return lax.all_gather(rows, "fsdp", axis=0, tiled=True, axis_index_groups=here.groups)


def scatter_line(here, rows):
    return lax.psum_scatter(
        rows, "fsdp", scatter_dimension=0, tiled=True, axis_index_groups=here.groups
    )


def carry_states(here, states, decays, backward):
    other_states, other_decays = here.over_core(states), here.over_core(decays)
    first = here.core == 0
    state_at = [jnp.where(first, states, other_states), jnp.where(first, other_states, states)]
    decay_at = [jnp.where(first, decays, other_decays), jnp.where(first, other_decays, decays)]
    order = [(j, c) for j in range(2) for c in range(2)]
    if backward:
        order = order[::-1]
    parts = [(state_at[c][j], decay_at[c][j]) for j, c in order]
    total, through = parts[0]
    for state, decay in parts[1:]:
        total = decay[:, None] * total + state
        through = through * decay
    half = total.shape[0] // 2
    mine = lax.dynamic_slice_in_dim(total, here.core * half, half, 0)
    mine_through = lax.dynamic_slice_in_dim(through, here.core * half, half, 0)
    row = jnp.pad(mine_through[None, :], ((0, 15), (0, total.shape[1] - half)))
    packed = jnp.concatenate([mine, row]).astype(BF16)
    entering = jnp.zeros_like(mine)
    for step in range(here.line_size - 1, 0, -1):
        came = here.along(packed, -step if backward else step).astype(F32)
        entering = came[half, :half][:, None] * entering + came[:half]
    entering = pair(here.core, entering, here.over_core(entering)).reshape(total.shape)
    at = {}
    for (j, c), (state, decay) in zip(order, parts):
        at[j, c] = entering
        entering = decay[:, None] * entering + state
    return jnp.where(
        first, jnp.stack([at[0, 0], at[1, 0]]), jnp.stack([at[0, 1], at[1, 1]])
    )


def on_device(
    tokens,
    attn_gain,
    w_query,
    w_key,
    w_value,
    w_down_rank,
    w_up_rank,
    gate_bias,
    w_outgate,
    head_gain,
    w_output,
    ffn_gain,
    w_gate,
    w_up,
    w_down,
    doc_starts,
    cotangent,
):
    here = Place()
    line = here.line_size
    tok, model = tokens.shape
    rows_d = w_query.shape[0]
    rows_f = w_down.shape[0]
    rank = w_up_rank.shape[0]
    cols_k = w_up_rank.shape[1]
    group = 4 * tok
    spans = group // SPAN
    per_seg = spans // 2
    me = 2 * here.seq + here.side

    def to_gathered(x):
        n = x.shape[0]
        return x.reshape(n, 2, line, 2, 2, rows_d).transpose(0, 2, 4, 1, 3, 5).reshape(n, model)

    def from_gathered(x):
        n = x.shape[0]
        return x.reshape(n, line, 2, 2, 2, rows_d).transpose(0, 3, 1, 4, 2, 5).reshape(n, model)

    small = jnp.concatenate(
        [
            attn_gain,
            ffn_gain,
            head_gain,
            gate_bias,
            w_up_rank.reshape(-1),
            w_down_rank.reshape(-1),
        ]
    )
    small_all = lax.all_gather(small, BOTH, axis=0)
    cuts = []
    at = 0
    for size in (rows_d, rows_d, head_gain.shape[0], cols_k, rank * cols_k, rows_d * rank):
        cuts.append(small_all[:, at : at + size])
        at += size
    devices = small_all.shape[0]
    full_attn_gain = cuts[0].reshape(model).astype(F32)
    full_ffn_gain = cuts[1].reshape(model).astype(F32)
    full_head_gain = cuts[2].reshape(HV).astype(F32)
    full_bias = cuts[3].reshape(HEADS * HK)
    full_up_rank = cuts[4].reshape(devices, rank, cols_k).transpose(1, 0, 2).reshape(rank, -1)
    full_down_rank = cuts[5].reshape(model, rank)
    my_bias = lax.dynamic_slice_in_dim(full_bias, me * HK, HK, 0).astype(F32)
    my_up_rank = lax.dynamic_slice_in_dim(full_up_rank, me * HK, HK, 1)
    down_rank_rows = (
        full_down_rank.reshape(2, line, 2, 2, rows_d, rank)
        .transpose(1, 3, 0, 2, 4, 5)
        .reshape(model, rank)
    )

    def heads_first(w, width):
        return w.reshape(rows_d, HEADS, width).transpose(1, 0, 2)

    mixer_cols = jnp.concatenate(
        [
            heads_first(w_query, HK),
            heads_first(w_key, HK),
            heads_first(w_value, HV),
            heads_first(w_outgate, HV),
        ],
        axis=2,
    )
    mixer_piece = exchange_quarters(here, mixer_cols)
    w_mixer = gather_line(here, mixer_piece.reshape(4 * rows_d, -1))

    def hidden_first(w):
        return (
            w.reshape(rows_d, 2, line, 2, 2, rows_f)
            .transpose(1, 3, 0, 2, 4, 5)
            .reshape(4, rows_d, -1)
        )

    quarter = 2 * line * rows_f
    ffn_cols = jnp.concatenate([hidden_first(w_gate), hidden_first(w_up)], axis=2)
    ffn_piece = exchange_quarters(here, ffn_cols)
    w_out = gather_line(here, here.swap_top(w_output))
    w_out = (
        w_out.reshape(2, line // 2, 2 * rows_d, model).transpose(1, 0, 2, 3).reshape(HV, model)
    )
    w_ffn = gather_line(here, ffn_piece.reshape(4 * rows_d, -1))
    w_dn = gather_line(here, w_down)

    inputs = tokens.astype(F32)
    scale_in = lax.rsqrt(jnp.mean(inputs * inputs, axis=-1, keepdims=True) + EPS)
    normed_in = (inputs * scale_in * full_attn_gain).astype(BF16)
    x_in = gather_tokens(here, to_gathered(normed_in))
    cot = gather_tokens(here, cotangent)
    other_docs = here.over_side(doc_starts)
    docs = pair(here.side, doc_starts, other_docs)
    flags = (jnp.arange(tok, dtype=jnp.int32) == docs[:, :, None]).astype(F32)
    flags = flags.reshape(spans, SPAN)

    projected = dot(x_in, w_mixer)
    queries = projected[:, :HK].astype(BF16)
    keys_in = projected[:, HK : 2 * HK].astype(BF16)
    values = projected[:, 2 * HK : 2 * HK + HV].astype(BF16)
    outgate = projected[:, 2 * HK + HV :]
    rank_low = dot(x_in, down_rank_rows).astype(BF16)
    logits = (dot(rank_low, my_up_rank) + my_bias).astype(BF16).astype(F32)

    decays = (jax.nn.log_sigmoid(logits) / GATE_SCALE).reshape(spans, SPAN, HK)
    causal = jnp.tril(jnp.ones((SPAN, SPAN), F32))
    running = jnp.einsum("ts,nsk->ntk", causal, decays, precision=lax.Precision.HIGHEST)
    count = jnp.einsum("ts,ns->nt", causal, flags, precision=lax.Precision.HIGHEST)
    closing = running[:, -1, :]
    unfinished = (count == 0.0)[:, :, None]
    tail = (count == count[:, -1:])[:, :, None]
    unbroken = count[:, -1:] == 0.0
    mask = (count[:, :, None] == count[:, None, :]) & (causal > 0)[None]
    q_s = queries.reshape(spans, SPAN, HK).astype(F32) * HK ** (-0.5)
    k_s = keys_in.reshape(spans, SPAN, HK).astype(F32)
    v_s = values.reshape(spans, SPAN, HV)
    grow = jnp.exp(running)
    shrink = jnp.exp(-running)
    to_end = jnp.where(tail, jnp.exp(closing[:, None, :] - running), 0.0)
    expanded = q_s * grow
    shrunk = k_s * shrink
    ending = k_s * to_end
    expanded_low = expanded.astype(BF16)
    shrunk_low = shrunk.astype(BF16)
    ending_low = ending.astype(BF16)
    reach_low = jnp.where(unfinished, expanded, 0.0).astype(BF16)
    scores = jnp.where(mask, ein("ntk,nsk->nts", expanded_low, shrunk_low), 0.0).astype(BF16)
    span_decay = jnp.where(unbroken, jnp.exp(closing), 0.0).reshape(2, per_seg, HK)
    updates = ein("ntk,ntv->nkv", ending_low, v_s).reshape(2, per_seg, HK, HV)

    before = [jnp.ones((2, HK), F32)]
    for c in range(per_seg):
        before.append(before[-1] * span_decay[:, c])
    through = before[-1]
    before = jnp.stack(before[:-1], axis=1)
    after = [jnp.ones((2, HK), F32)]
    for c in range(per_seg - 1, 0, -1):
        after.append(after[-1] * span_decay[:, c])
    after = jnp.stack(after[::-1], axis=1)
    seg_ending = (ending.reshape(2, per_seg, SPAN, HK) * after[:, :, None, :]).astype(BF16)
    seg_ending = seg_ending.reshape(2, per_seg * SPAN, HK)
    seg_values = values.reshape(2, per_seg * SPAN, HV)
    seg_end = ein("jtk,jtv->jkv", seg_ending, seg_values)
    entering = carry_states(here, seg_end, through, False)
    states = [entering]
    for c in range(per_seg - 1):
        states.append(span_decay[:, c, :, None] * states[-1] + updates[:, c])
    states = jnp.stack(states, axis=1).reshape(spans, HK, HV)
    states_low = states.astype(BF16)
    raw = ein("nts,nsv->ntv", scores, v_s) + ein("ntk,nkv->ntv", reach_low, states_low)
    mixed = raw.reshape(group, HV).astype(BF16).astype(F32)

    head_scale = lax.rsqrt(jnp.mean(mixed * mixed, axis=-1, keepdims=True) + EPS)
    normed_mix = mixed * head_scale * full_head_gain
    outgate_sig = jax.nn.sigmoid(outgate)
    gate_act = outgate * outgate_sig
    gated = (normed_mix * gate_act).astype(BF16)
    resid = inputs + scatter_tokens(here, dot(gated, w_out).astype(BF16))
    scale_mid = lax.rsqrt(jnp.mean(resid * resid, axis=-1, keepdims=True) + EPS)
    normed_mid = (resid * scale_mid * full_ffn_gain).astype(BF16)
    x_mid = gather_tokens(here, to_gathered(normed_mid))
    gate_up = dot(x_mid, w_ffn)
    gate_pre, up_pre = gate_up[:, :quarter], gate_up[:, quarter:]
    gate_sig = jax.nn.sigmoid(gate_pre)
    silu_gate = gate_pre * gate_sig
    hidden = (silu_gate * up_pre).astype(BF16)

    hidden_grad = dot_cols(cot, w_dn)
    gate_grad = (hidden_grad * up_pre * (gate_sig * (1.0 + gate_pre * (1.0 - gate_sig)))).astype(
        BF16
    )
    up_grad = (hidden_grad * silu_gate).astype(BF16)
    gate_up_grad = jnp.concatenate([gate_grad, up_grad], axis=1)
    mid_grad = scatter_tokens(here, dot_cols(gate_up_grad, w_ffn).astype(BF16))
    mid_grad = from_gathered(mid_grad)
    down_term = scatter_line(here, dot_rows(hidden, cot).astype(BF16))
    ffn_term = scatter_line(here, dot_rows(x_mid, gate_up_grad).astype(BF16))
    layer_output = (resid + scatter_tokens(here, dot(hidden, w_dn).astype(BF16))).astype(BF16)

    cot_here = cotangent.astype(F32)
    ffn_gain_term = jnp.sum(mid_grad * resid * scale_mid, axis=0)
    scaled_mid = full_ffn_gain * mid_grad
    resid_grad = (
        cot_here
        + scale_mid * scaled_mid
        - resid * scale_mid**3 * jnp.mean(scaled_mid * resid, axis=-1, keepdims=True)
    )
    branch = gather_tokens(here, resid_grad.astype(BF16))

    gated_grad = dot_cols(branch, w_out)
    outgate_grad = (
        gated_grad * normed_mix * outgate_sig * (1.0 + outgate * (1.0 - outgate_sig))
    ).astype(BF16)
    normed_grad = gated_grad * gate_act
    head_gain_term = jnp.sum(normed_grad * mixed * head_scale, axis=0)
    scaled_head = full_head_gain * normed_grad
    mixed_grad = (
        head_scale * scaled_head
        - mixed * head_scale**3 * jnp.mean(scaled_head * mixed, axis=-1, keepdims=True)
    ).astype(BF16)
    seg_reach = jnp.where(unfinished, expanded, 0.0).reshape(2, per_seg, SPAN, HK)
    seg_reach = (seg_reach * before[:, :, None, :]).astype(BF16)
    seg_reach = seg_reach.reshape(2, per_seg * SPAN, HK)
    start_grad = ein("jtk,jtv->jkv", seg_reach, mixed_grad.reshape(2, per_seg * SPAN, HV))
    leaving = carry_states(here, start_grad, through, True)
    out_term = dot_rows(gated, branch).astype(BF16)
    out_term = out_term.reshape(line // 2, 2, 2 * rows_d, model).transpose(1, 0, 2, 3)
    out_term = scatter_line(here, out_term.reshape(HV, model))

    o_g = mixed_grad.reshape(spans, SPAN, HV)
    reach_terms = ein("ntk,ntv->nkv", reach_low, o_g).reshape(2, per_seg, HK, HV)
    state_grads = [leaving]
    for c in range(per_seg - 1, 0, -1):
        state_grads.append(span_decay[:, c, :, None] * state_grads[-1] + reach_terms[:, c])
    state_grads = jnp.stack(state_grads[::-1], axis=1).reshape(spans, HK, HV)
    state_grads_low = state_grads.astype(BF16)
    score_grad = jnp.where(mask, ein("ntv,nsv->nts", o_g, v_s), 0.0).astype(BF16)
    expanded_grad = ein("nts,nsk->ntk", score_grad, shrunk_low) + jnp.where(
        unfinished, ein("ntv,nkv->ntk", o_g, states_low), 0.0
    )
    shrunk_grad = ein("nts,ntk->nsk", score_grad, expanded_low)
    ending_grad = ein("ntv,nkv->ntk", v_s, state_grads_low)
    value_grad = ein("nts,ntv->nsv", scores, o_g) + ein("ntk,nkv->ntv", ending_low, state_grads_low)
    query_grad = expanded_grad * grow * HK ** (-0.5)
    key_grad = shrunk_grad * shrink + ending_grad * to_end
    from_here = expanded * expanded_grad - shrunk * shrunk_grad
    from_past = ending * ending_grad
    carried = span_decay.reshape(spans, HK) * jnp.sum(states * state_grads, axis=-1)
    decay_grad = (
        jnp.einsum("ut,nuk->ntk", causal, from_here, precision=lax.Precision.HIGHEST)
        + jnp.einsum(
            "tu,nuk->ntk", causal - jnp.eye(SPAN), from_past, precision=lax.Precision.HIGHEST
        )
        + carried[:, None, :]
    )
    decay_grad = decay_grad * (1.0 - flags[:, :, None])
    logit_grad = (decay_grad.reshape(group, HK) * jax.nn.sigmoid(-logits) / GATE_SCALE).astype(BF16)
    grads = jnp.concatenate(
        [
            query_grad.reshape(group, HK).astype(BF16),
            key_grad.reshape(group, HK).astype(BF16),
            value_grad.reshape(group, HV).astype(BF16),
            outgate_grad,
        ],
        axis=1,
    )
    mixer_term = scatter_line(here, dot_rows(x_in, grads).astype(BF16))
    in_grad = scatter_tokens(here, dot_cols(grads, w_mixer).astype(BF16))
    in_grad = from_gathered(in_grad)

    bias_term = jnp.sum(logit_grad.astype(F32), axis=0)
    up_rank_term = dot_rows(rank_low, logit_grad)
    rank_part = dot_cols(logit_grad, my_up_rank)
    rank_part = rank_part + here.over_side(rank_part)
    rank_part = rank_part + here.over_seq(rank_part)
    position = (2 * here.side + here.seq) * tok
    rank_grad = lax.dynamic_slice_in_dim(rank_part, position, tok, 0).astype(BF16)
    down_rank_term = dot_rows(normed_in, rank_grad)
    in_grad = in_grad + dot_cols(rank_grad, full_down_rank)

    attn_gain_term = jnp.sum(in_grad * inputs * scale_in, axis=0)
    scaled_in = full_attn_gain * in_grad
    input_grad = (
        resid_grad
        + scale_in * scaled_in
        - inputs * scale_in**3 * jnp.mean(scaled_in * inputs, axis=-1, keepdims=True)
    ).astype(BF16)

    zero_bias = jnp.zeros((HEADS * HK,), F32)
    zero_up = jnp.zeros((rank, HEADS * HK), F32)
    bias_all = lax.dynamic_update_slice_in_dim(zero_bias, bias_term, me * HK, 0)
    up_all = lax.dynamic_update_slice_in_dim(zero_up, up_rank_term, me * HK, 1)
    small_terms = jnp.concatenate(
        [
            attn_gain_term.reshape(devices, -1),
            ffn_gain_term.reshape(devices, -1),
            head_gain_term.reshape(devices, -1),
            bias_all.reshape(devices, -1),
            up_all.reshape(rank, devices, cols_k).transpose(1, 0, 2).reshape(devices, -1),
            down_rank_term.reshape(devices, -1),
        ],
        axis=1,
    )
    small_sum = lax.psum_scatter(small_terms, BOTH, scatter_dimension=0, tiled=True)[0]
    pieces = []
    at = 0
    for size in (rows_d, rows_d, head_gain.shape[0], cols_k, rank * cols_k, rows_d * rank):
        pieces.append(small_sum[at : at + size])
        at += size

    down_grad = down_term.astype(F32)
    out_grad = here.swap_top(out_term).astype(F32)
    ffn_back = exchange_quarters(here, ffn_term.reshape(4, rows_d, 2 * quarter)).astype(F32)

    def hidden_last(g):
        return (
            g.reshape(2, 2, rows_d, line, 2, rows_f)
            .transpose(2, 0, 3, 1, 4, 5)
            .reshape(rows_d, 4 * quarter)
        )

    gate_out = hidden_last(ffn_back[:, :, :quarter])
    up_out = hidden_last(ffn_back[:, :, quarter:])
    mixer_back = exchange_quarters(here, mixer_term.reshape(4, rows_d, -1)).astype(F32)

    def heads_last(g):
        return g.transpose(1, 0, 2).reshape(rows_d, -1)

    query_out = heads_last(mixer_back[:, :, :HK])
    key_out = heads_last(mixer_back[:, :, HK : 2 * HK])
    value_out = heads_last(mixer_back[:, :, 2 * HK : 2 * HK + HV])
    outgate_out = heads_last(mixer_back[:, :, 2 * HK + HV :])
    return (
        layer_output,
        input_grad,
        pieces[0],
        query_out,
        key_out,
        value_out,
        pieces[5].reshape(rows_d, rank),
        pieces[4].reshape(rank, cols_k),
        pieces[3],
        outgate_out,
        pieces[2],
        out_grad,
        pieces[1],
        gate_out,
        up_out,
        down_grad,
    )


def solution(mesh):
    rows = P(BOTH, None)
    vector = P(BOTH)
    by_tokens = P(("fsdp", "seq"), None)
    by_cols = P(None, BOTH)
    in_specs = (
        by_tokens,
        vector,
        rows,
        rows,
        rows,
        rows,
        by_cols,
        vector,
        rows,
        vector,
        rows,
        vector,
        rows,
        rows,
        rows,
        P("fsdp"),
        by_tokens,
    )
    out_specs = (
        by_tokens,
        by_tokens,
        vector,
        rows,
        rows,
        rows,
        rows,
        by_cols,
        vector,
        rows,
        vector,
        rows,
        vector,
        rows,
        rows,
        rows,
    )
    return jax.shard_map(
        on_device, mesh=mesh, in_specs=in_specs, out_specs=out_specs, check_vma=False
    )
```

```python
import jax
import jax.numpy as jnp
from jax import lax
from jax.experimental import pallas as pl
from jax.experimental.pallas import tpu as pltpu
from jax.sharding import PartitionSpec as P

SPAN = 64
HK = 256
HV = 512
HEADS = 4
EPS = 1e-06
GATE_SCALE = 16.0
BOTH = ("seq", "fsdp")
F32 = jnp.float32
BF16 = jnp.bfloat16


def dot(left, right):
    return jnp.dot(left, right, preferred_element_type=F32)


def dot_rows(left, right):
    return lax.dot_general(left, right, (((0,), (0,)), ((), ())), preferred_element_type=F32)


def dot_cols(left, right):
    return lax.dot_general(left, right, (((1,), (1,)), ((), ())), preferred_element_type=F32)


def ein(form, left, right):
    return jnp.einsum(form, left, right, preferred_element_type=F32)


class Place:
    def __init__(self):
        self.fsdp = lax.axis_size("fsdp")
        self.line_size = self.fsdp // 4
        index = lax.axis_index("fsdp")
        self.seq = lax.axis_index("seq")
        self.core = index % 2
        self.side = (index // 2) % 2
        self.line = index // 4
        self.groups = [
            [4 * a + 2 * b + c for a in range(self.line_size) for c in range(2)] for b in range(2)
        ]

    def send(self, value, move, when=lambda a: True):
        pairs = []
        for s in range(2):
            for a in range(self.line_size):
                for b in range(2):
                    for c in range(2):
                        to = move(s, a, b, c)
                        if 0 <= to[1] < self.line_size and when(a):
                            source = s * self.fsdp + 4 * a + 2 * b + c
                            target = to[0] * self.fsdp + 4 * to[1] + 2 * to[2] + to[3]
                            pairs.append((source, target))
        return lax.ppermute(value, BOTH, pairs)

    def over_side(self, value):
        return self.send(value, lambda s, a, b, c: (s, a, 1 - b, c))

    def over_seq(self, value):
        return self.send(value, lambda s, a, b, c: (1 - s, a, b, c))

    def over_both(self, value):
        return self.send(value, lambda s, a, b, c: (1 - s, a, 1 - b, c))

    def over_core(self, value):
        return self.send(value, lambda s, a, b, c: (s, a, b, 1 - c))

    def along(self, value, step, when=lambda a: True):
        return self.send(value, lambda s, a, b, c: (s, a + step, b, c), when)

    def swap_top(self, value):
        half = self.line_size // 2
        return self.send(value, lambda s, a, b, c: (s, b * half + a % half, a // half, c))


def pair(which, own, other):
    first = which == 0
    return jnp.stack([jnp.where(first, own, other), jnp.where(first, other, own)])


def send_quarters(here, blocks):
    me = 2 * here.seq + here.side
    return (
        take(blocks, me),
        here.over_side(take(blocks, me ^ 1)),
        here.over_seq(take(blocks, me ^ 2)),
        here.over_both(take(blocks, me ^ 3)),
    )


def join_quarters(here, own, side, seq, both):
    rows = pair(here.seq, pair(here.side, own, side), pair(here.side, seq, both))
    return rows.reshape((4,) + own.shape)


def phase(*values):
    return lax.optimization_barrier(values)


def after(value, *others):
    return lax.optimization_barrier((value,) + others)[0]


def take(array, index, axis=0):
    return lax.dynamic_index_in_dim(array, index, axis, keepdims=False)


def near_halves(here, rows):
    half = rows.shape[0] // 2
    top, low = rows[:half], rows[half:]
    return jnp.stack([top, here.over_side(top)]), jnp.stack([low, here.over_seq(low)])


def far_halves(here, top_pair, low_pair):
    return here.over_seq(top_pair), here.over_side(low_pair)


def in_stream(here, top_pair, low_pair, top_far, low_far):
    own = jnp.stack([top_pair[0], low_pair[0]])
    side = jnp.stack([top_pair[1], low_far[0]])
    seq = jnp.stack([top_far[0], low_pair[1]])
    both = jnp.stack([top_far[1], low_far[1]])
    out = jnp.concatenate([pair(here.seq, own, seq), pair(here.seq, side, both)])
    return out.reshape(-1, out.shape[-1])


def gather_loose(here, rows):
    top_pair, low_pair = near_halves(here, rows)
    top_far, low_far = far_halves(here, top_pair, low_pair)
    parts = (top_pair, top_far, low_pair, low_far)
    return jnp.concatenate([p.reshape(-1, rows.shape[1]) for p in parts])


def in_loose(rows, side, seq, both):
    half = rows.shape[0] // 2
    top = [rows[:half], side[:half], seq[:half], both[:half]]
    low = [rows[half:], seq[half:], side[half:], both[half:]]
    return jnp.concatenate(top + low)


def near_sums(here, top, low):
    return top[:, 0], here.over_side(top[:, 1]), low[:, 0], here.over_seq(low[:, 1])


def far_sums(here, top, top_in, low, low_in):
    top_sum = top.astype(F32) + top_in.astype(F32)
    low_sum = low.astype(F32) + low_in.astype(F32)
    top_far = here.over_seq(top_sum[1].astype(BF16))
    low_far = here.over_side(low_sum[1].astype(BF16))
    return jnp.concatenate(
        [top_sum[0] + top_far.astype(F32), low_sum[0] + low_far.astype(F32)]
    )


def loose_parts(rows):
    parts = rows.reshape(2, 2, 2, -1, rows.shape[1])
    return parts[0], parts[1]


def stream_parts(here, rows):
    parts = rows.reshape(2, 2, 2, -1, rows.shape[1])
    own, other = take(parts, here.seq, 1), take(parts, 1 - here.seq, 1)
    top = jnp.stack([own[:, 0], other[:, 0]])
    low = jnp.stack([own[:, 1], other[:, 1]], axis=1)
    return top, low


def gather_line(here, rows):
    return lax.all_gather(rows, "fsdp", axis=0, tiled=True, axis_index_groups=here.groups)


def scatter_line(here, rows):
    return lax.psum_scatter(
        rows, "fsdp", scatter_dimension=0, tiled=True, axis_index_groups=here.groups
    )


def gather_small_plane(here, rows):
    rows = pair(here.side, rows, here.over_side(rows))
    rows = pair(here.seq, rows, here.over_seq(rows))
    return rows.transpose(0, 2, 1, 3, 4).reshape(2 * here.fsdp, -1)


def scatter_small_plane(here, rows):
    parts = rows.reshape(2, here.line_size, 2, 2, -1)
    parts = take(parts, here.seq) + here.over_seq(take(parts, 1 - here.seq))
    return take(parts, here.side, 1) + here.over_side(take(parts, 1 - here.side, 1))


def tile_order(line):
    pairs = []
    for q in range(2):
        for a in range(line):
            first = (q * line + a) * 2
            pairs.append(((first, first + 1), ((2 * a) * 2 + q, (2 * a + 1) * 2 + q)))
    return pairs


def swap_halves(first, second):
    left = lax.broadcasted_iota(jnp.int32, first.shape, 1) < 64
    low = jnp.where(left, first, pltpu.roll(second, 64, 1))
    high = jnp.where(left, pltpu.roll(first, 64, 1), second)
    return low, high


def columns(tile):
    return pl.ds(128 * tile, 128)


def rows_call(kernel, rows, outs, *arrays):
    block = 64
    count = rows // block

    def spec(shape):
        if shape[0] == rows:
            return pl.BlockSpec((block,) + shape[1:], lambda i: (i, 0))
        return pl.BlockSpec(shape, lambda i: (0, 0))

    moved = sum(a.size * a.dtype.itemsize for a in arrays)
    return pl.pallas_call(
        kernel,
        grid=(count,),
        in_specs=[spec(a.shape) for a in arrays],
        out_specs=[spec(shape) for shape, _ in outs],
        out_shape=[jax.ShapeDtypeStruct(*o) for o in outs],
        compiler_params=pltpu.CompilerParams(vmem_limit_bytes=32 * 2**20),
        cost_estimate=pl.CostEstimate(flops=0, bytes_accessed=2 * moved, transcendentals=0),
    )(*arrays)


def to_gathered(x, line):
    rows, model = x.shape
    size = model // (8 * line)
    if size != 64 or rows % 64:
        parts = x.reshape(rows, 2, line, 2, 2, size)
        return parts.transpose(0, 2, 4, 1, 3, 5).reshape(rows, model)

    def kernel(x_ref, out_ref):
        for (one, two), (low, high) in tile_order(line):
            got = swap_halves(
                x_ref[:, columns(one)].astype(F32), x_ref[:, columns(two)].astype(F32)
            )
            out_ref[:, columns(low)] = got[0].astype(out_ref.dtype)
            out_ref[:, columns(high)] = got[1].astype(out_ref.dtype)

    return rows_call(kernel, rows, [(x.shape, x.dtype)], x)[0]


def norm_forward(x, add, gain, line):
    rows, model = x.shape
    size = model // (8 * line)
    if size != 64 or rows % 64:
        total = x.astype(F32) + add
        scale = lax.rsqrt(jnp.mean(total * total, axis=-1, keepdims=True) + EPS)
        return total, to_gathered((total * scale * gain).astype(BF16), line)

    def kernel(x_ref, add_ref, gain_ref, total_ref, out_ref):
        total = x_ref[...].astype(F32) + add_ref[...]
        total_ref[...] = total
        scale = lax.rsqrt(jnp.mean(total * total, axis=-1, keepdims=True) + EPS)
        for (one, two), (low, high) in tile_order(line):
            cut = [
                total_ref[:, columns(t)] * scale * gain_ref[:, columns(t)] for t in (one, two)
            ]
            got = swap_halves(*cut)
            out_ref[:, columns(low)] = got[0].astype(BF16)
            out_ref[:, columns(high)] = got[1].astype(BF16)

    outs = [(x.shape, F32), (x.shape, BF16)]
    return rows_call(kernel, rows, outs, x, add, gain)


def norm_backward(grad, extra, x, base, gain, line, narrow):
    rows, model = x.shape
    size = model // (8 * line)
    plain = size != 64 or rows % 64 != 0
    if plain:
        parts = grad.reshape(rows, line, 2, 2, 2, size)
        grad = parts.transpose(0, 3, 1, 4, 2, 5).reshape(rows, model)

    def whole(grad, x, base, gain):
        x = x.astype(F32)
        scale = lax.rsqrt(jnp.mean(x * x, axis=-1, keepdims=True) + EPS)
        scaled = gain * grad
        mean = jnp.mean(scaled * x, axis=-1, keepdims=True)
        out = base.astype(F32) + scale * scaled - x * (scale * scale * scale * mean)
        return out, jnp.sum(grad * x * scale, axis=0, keepdims=True)

    if plain:
        out, term = whole(grad if extra is None else grad + extra, x, base, gain)
        return (out.astype(BF16), term) if narrow else (out, out.astype(BF16), term)

    def kernel(*refs):
        grad_ref, refs = refs[0], refs[1:]
        extra_ref = None
        if extra is not None:
            extra_ref, refs = refs[0], refs[1:]
        x_ref, base_ref, gain_ref, refs = refs[0], refs[1], refs[2], refs[3:]
        held_ref, term_ref, refs = refs[0], refs[1], refs[2:]
        for (one, two), (low, high) in tile_order(line):
            got = swap_halves(grad_ref[:, columns(low)], grad_ref[:, columns(high)])
            for tile, part in zip((one, two), got):
                if extra_ref is not None:
                    part = part + extra_ref[:, columns(tile)]
                held_ref[:, columns(tile)] = part
        out, term = whole(held_ref[...], x_ref[...], base_ref[...], gain_ref[...])
        held_ref[...] = out
        for ref in refs:
            ref[...] = out.astype(BF16)

        @pl.when(pl.program_id(0) == 0)
        def _():
            term_ref[...] = term

        @pl.when(pl.program_id(0) > 0)
        def _():
            term_ref[...] += term

    arrays = [grad] + ([] if extra is None else [extra]) + [x, base, gain]
    outs = [(x.shape, F32), ((1, model), F32), (x.shape, BF16)]
    wide, term, low = rows_call(kernel, rows, outs, *arrays)
    return (low, term) if narrow else (wide, low, term)


def in_side_order(here, two):
    return jnp.where(here.side == 0, two, two[::-1])


def carry_states(here, states, decays, backward):
    states, decays = in_side_order(here, states), in_side_order(here, decays)
    other_states = here.over_core(states.astype(BF16)).astype(F32)
    other_decays = here.over_core(decays)
    first = here.core == 0
    state_at = [jnp.where(first, states, other_states), jnp.where(first, other_states, states)]
    decay_at = [jnp.where(first, decays, other_decays), jnp.where(first, other_decays, decays)]
    order = [(j, c) for j in range(2) for c in range(2)]
    if backward:
        order = order[::-1]
    parts = [(state_at[c][j], decay_at[c][j]) for j, c in order]
    total, through = parts[0]
    for state, decay in parts[1:]:
        total = decay * total + state
        through = through * decay
    half = total.shape[0] // 2
    mine = lax.dynamic_slice_in_dim(total, here.core * half, half, 0)
    row = jnp.pad(through[None, :], ((0, 15), (0, 0)))
    packed = jnp.concatenate([mine, row]).astype(BF16)
    entering = jnp.zeros_like(mine)
    for step in range(here.line_size - 1, 0, -1):
        came = here.along(packed, -step if backward else step).astype(F32)
        entering = came[half] * entering + came[:half]
    entering = pair(here.core, entering, here.over_core(entering)).reshape(total.shape)
    at = {}
    for (j, c), (state, decay) in zip(order, parts):
        at[j, c] = entering
        entering = decay * entering + state
    out = jnp.where(first, jnp.stack([at[0, 0], at[1, 0]]), jnp.stack([at[0, 1], at[1, 1]]))
    return in_side_order(here, out)


def recurrence_backward(
    leaving, out_grad, values, expanded, shrunk, ending, scores, states, running, logits, decay,
    count, flags,
):
    spans, length, width = running.shape
    value_width = values.shape[-1]
    segments = leaving.shape[0]
    per_seg = spans // segments

    def kernel(
        leaving_ref, o_ref, v_ref, exp_ref, shr_ref, end_ref, score_ref, state_ref, run_ref,
        logit_ref, decay_ref, count_ref, row_ref, flag_ref, grads_ref, logit_grad_ref, carry,
    ):
        @pl.when(pl.program_id(1) == 0)
        def _():
            carry[...] = leaving_ref[0]

        def nt(a, b):
            return lax.dot_general(a, b, (((1,), (1,)), ((), ())), preferred_element_type=F32)

        def tn(a, b):
            return lax.dot_general(a, b, (((0,), (0,)), ((), ())), preferred_element_type=F32)

        o, v = o_ref[0], v_ref[0]
        expanded, shrunk, ending = exp_ref[0], shr_ref[0], end_ref[0]
        state, score = state_ref[0], score_ref[0]
        counts, count_row = count_ref[0], row_ref[0]
        unfinished = counts == 0.0
        tail = counts == counts[length - 1 :]
        above = lax.broadcasted_iota(jnp.int32, (length, length), 0)
        below = lax.broadcasted_iota(jnp.int32, (length, length), 1)
        mask = (counts == count_row) & (above >= below)
        later = carry[...]
        later_low = later.astype(BF16)

        score_grad = jnp.where(mask, nt(o, v), 0.0).astype(BF16)
        expanded_grad = dot(score_grad, shrunk) + jnp.where(unfinished, dot(o, state), 0.0)
        shrunk_grad = tn(score_grad, expanded)
        ending_grad = dot(v, later_low)
        value_grad = tn(score, o) + nt(ending, later_low)
        running = run_ref[0]
        to_end = jnp.where(tail, jnp.exp(running[length - 1 :] - running), 0.0)
        query_grad = expanded_grad * jnp.exp(running) * HK ** (-0.5)
        key_grad = shrunk_grad * jnp.exp(-running) + ending_grad * to_end
        grads_ref[:, :width] = query_grad.astype(BF16)
        grads_ref[:, width : 2 * width] = key_grad.astype(BF16)
        grads_ref[:, 2 * width :] = value_grad.astype(BF16)

        from_here = expanded.astype(F32) * expanded_grad - shrunk.astype(F32) * shrunk_grad
        from_past = ending.astype(F32) * ending_grad
        decay = decay_ref[0]
        carried = decay * jnp.sum(state.astype(F32) * later, axis=0, keepdims=True)
        upper = (below >= above).astype(F32)
        lower = (below < above).astype(F32)
        decay_grad = carried
        for triangle, terms in ((upper, from_here), (lower, from_past)):
            decay_grad = decay_grad + jnp.dot(
                triangle, terms, precision=lax.Precision.HIGHEST, preferred_element_type=F32
            )
        decay_grad = decay_grad * (1.0 - flag_ref[0])
        logits = logit_ref[0]
        logit_grad_ref[...] = (decay_grad * jax.nn.sigmoid(-logits) / GATE_SCALE).astype(BF16)

        reach = jnp.where(unfinished, expanded.astype(F32), 0.0).astype(BF16)
        carry[...] = decay * later + tn(o, reach)

    def at(j, c):
        return j * per_seg + per_seg - 1 - c

    def spec(array):
        return pl.BlockSpec((1,) + array.shape[1:], lambda j, c: (at(j, c), 0, 0))

    arrays = [
        out_grad, values, expanded, shrunk, ending, scores, states, running, logits,
        decay.reshape(spans, 1, width), count.reshape(spans, length, 1),
        count.reshape(spans, 1, length), flags.reshape(spans, length, 1),
    ]
    moved = sum(a.size * a.dtype.itemsize for a in arrays)
    tall = 2 * width + value_width
    return pl.pallas_call(
        kernel,
        grid=(segments, per_seg),
        in_specs=[pl.BlockSpec((1, value_width, width), lambda j, c: (j, 0, 0))]
        + [spec(a) for a in arrays],
        out_specs=[
            pl.BlockSpec((length, tall), lambda j, c: (at(j, c), 0)),
            pl.BlockSpec((length, width), lambda j, c: (at(j, c), 0)),
        ],
        out_shape=[
            jax.ShapeDtypeStruct((spans * length, tall), BF16),
            jax.ShapeDtypeStruct((spans * length, width), BF16),
        ],
        scratch_shapes=[pltpu.VMEM((value_width, width), F32)],
        compiler_params=pltpu.CompilerParams(vmem_limit_bytes=32 * 2**20),
        cost_estimate=pl.CostEstimate(
            flops=10 * spans * length * width * value_width,
            bytes_accessed=moved,
            transcendentals=4 * running.size,
        ),
    )(leaving, *arrays)


def on_device(
    tokens,
    attn_gain,
    w_query,
    w_key,
    w_value,
    w_down_rank,
    w_up_rank,
    gate_bias,
    w_outgate,
    head_gain,
    w_output,
    ffn_gain,
    w_gate,
    w_up,
    w_down,
    doc_starts,
    cotangent,
):
    here = Place()
    line = here.line_size
    tok, model = tokens.shape
    rows_d = w_query.shape[0]
    rows_f = w_down.shape[0]
    rank = w_up_rank.shape[0]
    cols_k = w_up_rank.shape[1]
    group = 4 * tok
    spans = group // SPAN
    per_seg = spans // 2
    me = 2 * here.seq + here.side

    small = jnp.concatenate(
        [
            attn_gain,
            ffn_gain,
            head_gain,
            gate_bias,
            w_up_rank.reshape(-1),
            w_down_rank.reshape(-1),
        ]
    )
    small_size = small.shape[0]
    small_rows = 8 * -(-small_size // (8 * model))
    small = jnp.pad(small, (0, small_rows * model - small_size)).reshape(small_rows, model)
    out_lines = gather_line(here, jnp.concatenate([here.swap_top(w_output), small]))
    out_lines = out_lines.reshape(line, 2, rows_d + small_rows, model)
    small_line = out_lines[:, :, rows_d:].reshape(line, 2, -1)[:, :, :small_size]
    w_out = out_lines[:, :, :rows_d].reshape(2, line // 2, 2 * rows_d, model)
    w_out = w_out.transpose(1, 0, 2, 3).reshape(HV, model)

    def heads_first(w, width):
        return w.reshape(rows_d, HEADS, width).transpose(1, 0, 2)

    def hidden_first(w):
        return (
            w.reshape(rows_d, 2, line, 2, 2, rows_f)
            .transpose(1, 3, 0, 2, 4, 5)
            .reshape(4, rows_d, -1)
        )

    quarter = 2 * line * rows_f
    mixer_cols = jnp.concatenate(
        [
            heads_first(w_query, HK),
            heads_first(w_key, HK),
            heads_first(w_value, HV),
            heads_first(w_outgate, HV),
        ],
        axis=2,
    )
    *mixer_quarters, tokens_in, w_gate, w_up = phase(
        *send_quarters(here, mixer_cols), to_gathered(tokens, line), w_gate, w_up
    )
    mixer_piece = join_quarters(here, *mixer_quarters).reshape(4 * rows_d, -1)
    w_mixer = gather_line(here, mixer_piece)
    other_docs = here.over_side(doc_starts)
    top_pair, low_pair, small_line, gate_cols, other_docs, w_up = phase(
        *near_halves(here, tokens_in), small_line, hidden_first(w_gate), other_docs, w_up
    )
    small_all = gather_small_plane(here, small_line)
    small_all, top_pair, low_pair, up_cols = phase(
        small_all, top_pair, low_pair, hidden_first(w_up)
    )
    ffn_cols = jnp.concatenate([gate_cols, up_cols], axis=2)
    top_far, low_far, ffn_cols, top_pair, low_pair = phase(
        *far_halves(here, top_pair, low_pair), ffn_cols, top_pair, low_pair
    )
    ffn_quarters = send_quarters(here, ffn_cols)
    wide_in = in_stream(here, top_pair, low_pair, top_far, low_far).astype(F32)
    cuts = []
    at = 0
    for size in (rows_d, rows_d, head_gain.shape[0], cols_k, rank * cols_k, rows_d * rank):
        cuts.append(small_all[:, at : at + size])
        at += size
    devices = small_all.shape[0]
    full_attn_gain = cuts[0].reshape(model).astype(F32)
    full_ffn_gain = cuts[1].reshape(model).astype(F32)
    full_head_gain = cuts[2].reshape(HV).astype(F32)
    full_bias = cuts[3].reshape(HEADS * HK)
    full_up_rank = cuts[4].reshape(devices, rank, cols_k).transpose(1, 0, 2).reshape(rank, -1)
    full_down_rank = cuts[5].reshape(model, rank)
    my_bias = lax.dynamic_slice_in_dim(full_bias, me * HK, HK, 0).astype(F32)
    my_up_rank = lax.dynamic_slice_in_dim(full_up_rank, me * HK, HK, 1)
    down_rank_rows = (
        full_down_rank.reshape(2, line, 2, 2, rows_d, rank)
        .transpose(1, 3, 0, 2, 4, 5)
        .reshape(model, rank)
    )

    wide_scale = lax.rsqrt(jnp.mean(wide_in * wide_in, axis=-1, keepdims=True) + EPS)
    x_in = (wide_in * wide_scale * to_gathered(full_attn_gain[None], line)).astype(BF16)
    rank_low = dot(x_in, down_rank_rows).astype(BF16)
    *ffn_quarters, x_in, rank_low, cotangent, w_down = phase(
        *ffn_quarters, x_in, rank_low, cotangent, w_down
    )
    ffn_piece = join_quarters(here, *ffn_quarters).reshape(4 * rows_d, -1)
    w_ffn = gather_line(here, ffn_piece)
    w_dn = gather_line(here, after(w_down, ffn_piece))
    cot_parts = here.over_side(cotangent), here.over_seq(cotangent), here.over_both(cotangent)

    inputs = tokens.astype(F32)
    scale_in = lax.rsqrt(jnp.mean(inputs * inputs, axis=-1, keepdims=True) + EPS)
    normed_in = (inputs * scale_in * full_attn_gain).astype(BF16)
    docs = jnp.stack([doc_starts, other_docs])
    flags = (jnp.arange(tok, dtype=jnp.int32) == docs[:, :, None]).astype(F32)
    flags = flags.reshape(spans, SPAN)

    projected = dot(x_in, w_mixer)
    queries = projected[:, :HK].astype(BF16)
    keys_in = projected[:, HK : 2 * HK].astype(BF16)
    values = projected[:, 2 * HK : 2 * HK + HV].astype(BF16)
    outgate = projected[:, 2 * HK + HV :]
    logits = (dot(rank_low, my_up_rank) + my_bias).astype(BF16).astype(F32)

    decays = (jax.nn.log_sigmoid(logits) / GATE_SCALE).reshape(spans, SPAN, HK)
    causal = jnp.tril(jnp.ones((SPAN, SPAN), F32))
    running = jnp.einsum("ts,nsk->ntk", causal, decays, precision=lax.Precision.HIGHEST)
    count = jnp.einsum("ts,ns->nt", causal, flags, precision=lax.Precision.HIGHEST)
    closing = running[:, -1, :]
    unfinished = (count == 0.0)[:, :, None]
    tail = (count == count[:, -1:])[:, :, None]
    unbroken = count[:, -1:] == 0.0
    mask = (count[:, :, None] == count[:, None, :]) & (causal > 0)[None]
    q_s = queries.reshape(spans, SPAN, HK).astype(F32) * HK ** (-0.5)
    k_s = keys_in.reshape(spans, SPAN, HK).astype(F32)
    v_s = values.reshape(spans, SPAN, HV)
    grow = jnp.exp(running)
    shrink = jnp.exp(-running)
    to_end = jnp.where(tail, jnp.exp(closing[:, None, :] - running), 0.0)
    expanded = q_s * grow
    shrunk = k_s * shrink
    ending = k_s * to_end
    expanded_low = expanded.astype(BF16)
    shrunk_low = shrunk.astype(BF16)
    ending_low = ending.astype(BF16)
    reach_low = jnp.where(unfinished, expanded, 0.0).astype(BF16)
    exact = lax.Precision.HIGHEST
    wide_scores = jnp.einsum("ntk,nsk->nts", expanded, shrunk, precision=exact)
    wide_scores = jnp.where(mask, wide_scores, 0.0)
    scores = wide_scores.astype(BF16)
    span_decay = jnp.where(unbroken, jnp.exp(closing), 0.0).reshape(2, per_seg, HK)
    updates = ein("ntv,ntk->nvk", v_s, ending_low).reshape(2, per_seg, HV, HK)

    before = [jnp.ones((2, HK), F32)]
    for c in range(per_seg):
        before.append(before[-1] * span_decay[:, c])
    through = before[-1]
    before = jnp.stack(before[:-1], axis=1)
    rest = [jnp.ones((2, HK), F32)]
    for c in range(per_seg - 1, 0, -1):
        rest.append(rest[-1] * span_decay[:, c])
    rest = jnp.stack(rest[::-1], axis=1)
    seg_ending = (ending.reshape(2, per_seg, SPAN, HK) * rest[:, :, None, :]).astype(BF16)
    seg_ending = seg_ending.reshape(2, per_seg * SPAN, HK)
    seg_values = values.reshape(2, per_seg * SPAN, HV)
    seg_end = ein("jtv,jtk->jvk", seg_values, seg_ending)
    *cot_parts, seg_end = phase(*cot_parts, seg_end)
    cot = in_loose(cotangent, *cot_parts)
    entering = carry_states(here, seg_end, through, False)
    states = [entering]
    for c in range(per_seg - 1):
        states.append(span_decay[:, c, None, :] * states[-1] + updates[:, c])
    states_low = jnp.stack([s.astype(BF16) for s in states], axis=1).reshape(spans, HV, HK)
    inside = jnp.einsum("nts,nsv->ntv", wide_scores, v_s.astype(F32), precision=exact)
    raw = inside + ein("ntk,nvk->ntv", reach_low, states_low)
    mixed = raw.reshape(group, HV).astype(BF16).astype(F32)

    head_scale = lax.rsqrt(jnp.mean(mixed * mixed, axis=-1, keepdims=True) + EPS)
    normed_mix = mixed * head_scale * full_head_gain
    outgate_sig = jax.nn.sigmoid(outgate)
    gate_act = outgate * outgate_sig
    gated = (normed_mix * gate_act).astype(BF16)
    branch_parts = near_sums(here, *stream_parts(here, dot(gated, w_out).astype(BF16)))
    branch_out = far_sums(here, *branch_parts)
    resid, normed_mid = norm_forward(tokens, branch_out, full_ffn_gain[None], line)
    x_mid = gather_loose(here, normed_mid)
    gate_up = dot(x_mid, w_ffn)
    gate_pre, up_pre = gate_up[:, :quarter], gate_up[:, quarter:]
    gate_sig = jax.nn.sigmoid(gate_pre)
    silu_gate = gate_pre * gate_sig
    hidden = (silu_gate * up_pre).astype(BF16)

    down_part = dot_rows(hidden, cot).astype(BF16)
    down_term = scatter_line(here, down_part)
    hidden_grad = dot_cols(after(cot, down_part), w_dn)
    gate_grad = (hidden_grad * up_pre * (gate_sig * (1.0 + gate_pre * (1.0 - gate_sig)))).astype(
        BF16
    )
    up_grad = (hidden_grad * silu_gate).astype(BF16)
    gate_up_grad = jnp.concatenate([gate_grad, up_grad], axis=1)
    mid_parts = near_sums(here, *loose_parts(dot_cols(gate_up_grad, w_ffn).astype(BF16)))
    ffn_part = dot_rows(x_mid, gate_up_grad).astype(BF16)
    *mid_parts, ffn_part = phase(*mid_parts, ffn_part)
    mid_grad, down_term, ffn_part, hidden = phase(
        far_sums(here, *mid_parts), down_term, ffn_part, hidden
    )
    ffn_term = scatter_line(here, ffn_part)
    resid_grad, branch, ffn_gain_term = norm_backward(
        mid_grad, None, resid, cotangent, full_ffn_gain[None], line, False
    )
    near = near_halves(here, branch)
    *near, hidden = phase(*near, hidden)
    down_out = dot(hidden, w_dn).astype(BF16)
    *far, down_out = phase(*far_halves(here, *near), down_out)
    branch = in_stream(here, *near, *far)

    gated_grad = dot_cols(branch, w_out)
    outgate_grad = (
        gated_grad * normed_mix * outgate_sig * (1.0 + outgate * (1.0 - outgate_sig))
    ).astype(BF16)
    normed_grad = gated_grad * gate_act
    head_gain_term = jnp.sum(normed_grad * mixed * head_scale, axis=0)
    scaled_head = full_head_gain * normed_grad
    mixed_grad = (
        head_scale * scaled_head
        - mixed * head_scale**3 * jnp.mean(scaled_head * mixed, axis=-1, keepdims=True)
    ).astype(BF16)
    seg_reach = jnp.where(unfinished, expanded, 0.0).reshape(2, per_seg, SPAN, HK)
    seg_reach = (seg_reach * before[:, :, None, :]).astype(BF16)
    seg_reach = seg_reach.reshape(2, per_seg * SPAN, HK)
    start_grad = ein("jtv,jtk->jvk", mixed_grad.reshape(2, per_seg * SPAN, HV), seg_reach)
    leaving = carry_states(here, start_grad, through, True)
    down_parts = near_sums(here, *loose_parts(after(down_out, start_grad)))
    out_term = dot_rows(gated, branch).astype(BF16)
    out_term = out_term.reshape(line // 2, 2, 2 * rows_d, model).transpose(1, 0, 2, 3)
    out_part = out_term.reshape(HV, model)
    leaving, out_part, *down_parts = phase(leaving, out_part, *down_parts)
    layer_output = (resid + far_sums(here, *down_parts)).astype(BF16)
    out_term = scatter_line(here, after(out_part, ffn_term))

    mixer_grads, logit_grad = recurrence_backward(
        leaving,
        mixed_grad.reshape(spans, SPAN, HV),
        v_s,
        expanded_low,
        shrunk_low,
        ending_low,
        scores,
        states_low,
        running,
        logits.reshape(spans, SPAN, HK),
        span_decay,
        count,
        flags,
    )
    mixer_grads, layer_output = phase(mixer_grads, layer_output)
    grads = jnp.concatenate([mixer_grads, outgate_grad], axis=1)
    in_part = dot_cols(grads, w_mixer).astype(BF16)

    bias_term = jnp.sum(logit_grad.astype(F32), axis=0)
    up_rank_term = dot_rows(rank_low, logit_grad)
    rank_part = dot_cols(logit_grad, my_up_rank)
    other_side = here.over_side(rank_part[2 * tok :])
    rank_part = rank_part[: 2 * tok] + other_side
    rank_part = rank_part + here.over_seq(rank_part)
    rank_grad = lax.dynamic_slice_in_dim(rank_part, here.seq * tok, tok, 0).astype(BF16)
    down_rank_term = dot_rows(normed_in, rank_grad)
    rank_in_grad = dot_cols(rank_grad, full_down_rank)
    attn_gain_here = jnp.sum(in_part.astype(F32) * (wide_in * wide_scale), axis=0)
    attn_gain_term = jnp.sum(rank_in_grad * (inputs * scale_in), axis=0)

    zero_bias = jnp.zeros((HEADS * HK,), F32)
    zero_up = jnp.zeros((rank, HEADS * HK), F32)
    bias_all = lax.dynamic_update_slice_in_dim(zero_bias, bias_term, me * HK, 0)
    up_all = lax.dynamic_update_slice_in_dim(zero_up, up_rank_term, me * HK, 1)
    small_terms = jnp.concatenate(
        [
            attn_gain_term.reshape(devices, -1)
            + attn_gain_here.reshape(line, 2, 2, 2, rows_d)
            .transpose(2, 0, 3, 1, 4)
            .reshape(devices, -1),
            ffn_gain_term.reshape(devices, -1),
            head_gain_term.reshape(devices, -1),
            bias_all.reshape(devices, -1),
            up_all.reshape(rank, devices, cols_k).transpose(1, 0, 2).reshape(devices, -1),
            down_rank_term.reshape(devices, -1),
        ],
        axis=1,
    )
    small_part = scatter_small_plane(here, small_terms)
    in_parts = near_sums(here, *stream_parts(here, after(in_part, small_part)))
    small_cols = 128 * -(-small_size // (512 * rows_d))
    small_part = jnp.pad(
        small_part.reshape(2 * line, small_size),
        ((0, 0), (0, 4 * rows_d * small_cols - small_size)),
    ).reshape(-1, small_cols)
    wide_grads = jnp.pad(grads, ((0, 0), (0, small_cols)))
    mixer_part = dot_rows(x_in, after(wide_grads, in_part)).astype(BF16)
    mixer_part = lax.dynamic_update_slice(mixer_part, small_part.astype(BF16), (0, grads.shape[1]))
    mixer_part, ffn_term, out_term = phase(mixer_part, ffn_term, out_term)
    mixer_term = scatter_line(here, mixer_part)
    *in_parts, ffn_term = phase(*in_parts, ffn_term)
    in_grad = far_sums(here, *in_parts)
    ffn_back = send_quarters(here, ffn_term.reshape(4, rows_d, 2 * quarter))

    input_grad, _ = norm_backward(
        in_grad,
        rank_in_grad,
        tokens,
        resid_grad,
        full_attn_gain[None],
        line,
        True,
    )

    down_grad = down_term.astype(F32)
    out_grad = here.swap_top(out_term).astype(F32)
    input_grad, out_grad, *ffn_back = phase(input_grad, out_grad, *ffn_back)
    ffn_back = join_quarters(here, *ffn_back).astype(F32)

    def hidden_last(g):
        return (
            g.reshape(2, 2, rows_d, line, 2, rows_f)
            .transpose(2, 0, 3, 1, 4, 5)
            .reshape(rows_d, 4 * quarter)
        )

    gate_out = hidden_last(ffn_back[:, :, :quarter])
    up_out = hidden_last(ffn_back[:, :, quarter:])
    small_sum = mixer_term[:, 2 * HK + 2 * HV :].reshape(-1).astype(F32)
    mixer_term = after(mixer_term[:, : 2 * HK + 2 * HV], gate_out, up_out, out_grad, down_grad)
    mixer_back = send_quarters(here, mixer_term.reshape(4, rows_d, -1))
    mixer_back = join_quarters(here, *mixer_back).astype(F32)

    def heads_last(g):
        return g.transpose(1, 0, 2).reshape(rows_d, -1)

    query_out = heads_last(mixer_back[:, :, :HK])
    key_out = heads_last(mixer_back[:, :, HK : 2 * HK])
    value_out = heads_last(mixer_back[:, :, 2 * HK : 2 * HK + HV])
    outgate_out = heads_last(mixer_back[:, :, 2 * HK + HV :])
    small_sum = after(small_sum, query_out, key_out, value_out, outgate_out)
    pieces = []
    at = 0
    for size in (rows_d, rows_d, head_gain.shape[0], cols_k, rank * cols_k, rows_d * rank):
        pieces.append(small_sum[at : at + size])
        at += size
    return (
        layer_output,
        input_grad,
        pieces[0],
        query_out,
        key_out,
        value_out,
        pieces[5].reshape(rows_d, rank),
        pieces[4].reshape(rank, cols_k),
        pieces[3],
        outgate_out,
        pieces[2],
        out_grad,
        pieces[1],
        gate_out,
        up_out,
        down_grad,
    )


def solution(mesh):
    rows = P(BOTH, None)
    vector = P(BOTH)
    by_tokens = P(("fsdp", "seq"), None)
    by_cols = P(None, BOTH)
    in_specs = (
        by_tokens,
        vector,
        rows,
        rows,
        rows,
        rows,
        by_cols,
        vector,
        rows,
        vector,
        rows,
        vector,
        rows,
        rows,
        rows,
        P("fsdp"),
        by_tokens,
    )
    out_specs = (
        by_tokens,
        by_tokens,
        vector,
        rows,
        rows,
        rows,
        rows,
        by_cols,
        vector,
        rows,
        vector,
        rows,
        vector,
        rows,
        rows,
        rows,
    )
    return jax.shard_map(
        on_device, mesh=mesh, in_specs=in_specs, out_specs=out_specs, check_vma=False
    )
```

```python
import jax
import jax.numpy as jnp
from jax import lax
from jax.experimental import pallas as pl
from jax.experimental.pallas import tpu as pltpu
from jax.sharding import PartitionSpec as P

SPAN = 64
HK = 256
HV = 512
HEADS = 4
EPS = 1e-06
GATE_SCALE = 16.0
BOTH = ("seq", "fsdp")
F32 = jnp.float32
BF16 = jnp.bfloat16


def dot(left, right):
    return jnp.dot(left, right, preferred_element_type=F32)


def dot_rows(left, right):
    return lax.dot_general(left, right, (((0,), (0,)), ((), ())), preferred_element_type=F32)


def dot_cols(left, right):
    return lax.dot_general(left, right, (((1,), (1,)), ((), ())), preferred_element_type=F32)


def ein(form, left, right):
    return jnp.einsum(form, left, right, preferred_element_type=F32)


class Place:
    def __init__(self):
        self.fsdp = lax.axis_size("fsdp")
        self.line_size = self.fsdp // 4
        index = lax.axis_index("fsdp")
        self.seq = lax.axis_index("seq")
        self.core = index % 2
        self.side = (index // 2) % 2
        self.line = index // 4
        self.groups = [
            [4 * a + 2 * b + c for a in range(self.line_size) for c in range(2)] for b in range(2)
        ]

    def send(self, value, move, when=lambda a: True):
        pairs = []
        for s in range(2):
            for a in range(self.line_size):
                for b in range(2):
                    for c in range(2):
                        to = move(s, a, b, c)
                        if 0 <= to[1] < self.line_size and when(a):
                            source = s * self.fsdp + 4 * a + 2 * b + c
                            target = to[0] * self.fsdp + 4 * to[1] + 2 * to[2] + to[3]
                            pairs.append((source, target))
        return lax.ppermute(value, BOTH, pairs)

    def over_side(self, value):
        return self.send(value, lambda s, a, b, c: (s, a, 1 - b, c))

    def over_seq(self, value):
        return self.send(value, lambda s, a, b, c: (1 - s, a, b, c))

    def over_both(self, value):
        return self.send(value, lambda s, a, b, c: (1 - s, a, 1 - b, c))

    def over_core(self, value):
        return self.send(value, lambda s, a, b, c: (s, a, b, 1 - c))

    def along(self, value, step, when=lambda a: True):
        return self.send(value, lambda s, a, b, c: (s, a + step, b, c), when)

    def swap_top(self, value):
        half = self.line_size // 2
        return self.send(value, lambda s, a, b, c: (s, b * half + a % half, a // half, c))


def pair(which, own, other):
    first = which == 0
    return jnp.stack([jnp.where(first, own, other), jnp.where(first, other, own)])


def send_quarters(here, blocks):
    me = 2 * here.seq + here.side
    return (
        take(blocks, me),
        here.over_side(take(blocks, me ^ 1)),
        here.over_seq(take(blocks, me ^ 2)),
        here.over_both(take(blocks, me ^ 3)),
    )


def join_quarters(here, own, side, seq, both):
    rows = pair(here.seq, pair(here.side, own, side), pair(here.side, seq, both))
    return rows.reshape((4,) + own.shape)


def phase(*values):
    return lax.optimization_barrier(values)


def after(value, *others):
    return lax.optimization_barrier((value,) + others)[0]


def take(array, index, axis=0):
    return lax.dynamic_index_in_dim(array, index, axis, keepdims=False)


def near_halves(here, rows):
    half = rows.shape[0] // 2
    top, low = rows[:half], rows[half:]
    return jnp.stack([top, here.over_side(top)]), jnp.stack([low, here.over_seq(low)])


def far_halves(here, top_pair, low_pair):
    return here.over_seq(top_pair), here.over_side(low_pair)


def in_stream(here, top_pair, low_pair, top_far, low_far):
    own = jnp.stack([top_pair[0], low_pair[0]])
    side = jnp.stack([top_pair[1], low_far[0]])
    seq = jnp.stack([top_far[0], low_pair[1]])
    both = jnp.stack([top_far[1], low_far[1]])
    out = jnp.concatenate([pair(here.seq, own, seq), pair(here.seq, side, both)])
    return out.reshape(-1, out.shape[-1])


def gather_loose(here, rows):
    top_pair, low_pair = near_halves(here, rows)
    top_far, low_far = far_halves(here, top_pair, low_pair)
    parts = (top_pair, top_far, low_pair, low_far)
    return jnp.concatenate([p.reshape(-1, rows.shape[1]) for p in parts])


def in_loose(rows, side, seq, both):
    half = rows.shape[0] // 2
    top = [rows[:half], side[:half], seq[:half], both[:half]]
    low = [rows[half:], seq[half:], side[half:], both[half:]]
    return jnp.concatenate(top + low)


def near_sums(here, top, low):
    return top[:, 0], here.over_side(top[:, 1]), low[:, 0], here.over_seq(low[:, 1])


def far_sums(here, top, top_in, low, low_in):
    top_sum = top.astype(F32) + top_in.astype(F32)
    low_sum = low.astype(F32) + low_in.astype(F32)
    top_far = here.over_seq(top_sum[1].astype(BF16))
    low_far = here.over_side(low_sum[1].astype(BF16))
    return jnp.concatenate(
        [top_sum[0] + top_far.astype(F32), low_sum[0] + low_far.astype(F32)]
    )


def loose_parts(rows):
    parts = rows.reshape(2, 2, 2, -1, rows.shape[1])
    return parts[0], parts[1]


def stream_parts(here, rows):
    parts = rows.reshape(2, 2, 2, -1, rows.shape[1])
    own, other = take(parts, here.seq, 1), take(parts, 1 - here.seq, 1)
    top = jnp.stack([own[:, 0], other[:, 0]])
    low = jnp.stack([own[:, 1], other[:, 1]], axis=1)
    return top, low


def gather_line(here, rows):
    return lax.all_gather(rows, "fsdp", axis=0, tiled=True, axis_index_groups=here.groups)


def scatter_line(here, rows):
    return lax.psum_scatter(
        rows, "fsdp", scatter_dimension=0, tiled=True, axis_index_groups=here.groups
    )


def gather_small_plane(here, rows):
    rows = pair(here.side, rows, here.over_side(rows))
    rows = pair(here.seq, rows, here.over_seq(rows))
    return rows.transpose(0, 2, 1, 3, 4).reshape(2 * here.fsdp, -1)


def scatter_small_plane(here, rows):
    parts = rows.reshape(2, here.line_size, 2, 2, -1)
    parts = take(parts, here.seq) + here.over_seq(take(parts, 1 - here.seq))
    return take(parts, here.side, 1) + here.over_side(take(parts, 1 - here.side, 1))


def tile_order(line):
    pairs = []
    for q in range(2):
        for a in range(line):
            first = (q * line + a) * 2
            pairs.append(((first, first + 1), ((2 * a) * 2 + q, (2 * a + 1) * 2 + q)))
    return pairs


def swap_halves(first, second):
    left = lax.broadcasted_iota(jnp.int32, first.shape, 1) < 64
    low = jnp.where(left, first, pltpu.roll(second, 64, 1))
    high = jnp.where(left, pltpu.roll(first, 64, 1), second)
    return low, high


def columns(tile):
    return pl.ds(128 * tile, 128)


def rows_call(kernel, rows, outs, *arrays):
    block = 64
    count = rows // block

    def spec(shape):
        if shape[0] == rows:
            return pl.BlockSpec((block,) + shape[1:], lambda i: (i, 0))
        return pl.BlockSpec(shape, lambda i: (0, 0))

    moved = sum(a.size * a.dtype.itemsize for a in arrays)
    return pl.pallas_call(
        kernel,
        grid=(count,),
        in_specs=[spec(a.shape) for a in arrays],
        out_specs=[spec(shape) for shape, _ in outs],
        out_shape=[jax.ShapeDtypeStruct(*o) for o in outs],
        compiler_params=pltpu.CompilerParams(vmem_limit_bytes=32 * 2**20),
        cost_estimate=pl.CostEstimate(flops=0, bytes_accessed=2 * moved, transcendentals=0),
    )(*arrays)


def to_gathered(x, line):
    rows, model = x.shape
    size = model // (8 * line)
    if size != 64 or rows % 64:
        parts = x.reshape(rows, 2, line, 2, 2, size)
        return parts.transpose(0, 2, 4, 1, 3, 5).reshape(rows, model)

    def kernel(x_ref, out_ref):
        for (one, two), (low, high) in tile_order(line):
            got = swap_halves(
                x_ref[:, columns(one)].astype(F32), x_ref[:, columns(two)].astype(F32)
            )
            out_ref[:, columns(low)] = got[0].astype(out_ref.dtype)
            out_ref[:, columns(high)] = got[1].astype(out_ref.dtype)

    return rows_call(kernel, rows, [(x.shape, x.dtype)], x)[0]


def norm_forward(x, add, gain, line):
    rows, model = x.shape
    size = model // (8 * line)
    if size != 64 or rows % 64:
        total = x.astype(F32) + add
        scale = lax.rsqrt(jnp.mean(total * total, axis=-1, keepdims=True) + EPS)
        return total, to_gathered((total * scale * gain).astype(BF16), line)

    def kernel(x_ref, add_ref, gain_ref, total_ref, out_ref):
        total = x_ref[...].astype(F32) + add_ref[...]
        total_ref[...] = total
        scale = lax.rsqrt(jnp.mean(total * total, axis=-1, keepdims=True) + EPS)
        for (one, two), (low, high) in tile_order(line):
            cut = [
                total_ref[:, columns(t)] * scale * gain_ref[:, columns(t)] for t in (one, two)
            ]
            got = swap_halves(*cut)
            out_ref[:, columns(low)] = got[0].astype(BF16)
            out_ref[:, columns(high)] = got[1].astype(BF16)

    outs = [(x.shape, F32), (x.shape, BF16)]
    return rows_call(kernel, rows, outs, x, add, gain)


def norm_backward(grad, extra, x, base, gain, line, narrow):
    rows, model = x.shape
    size = model // (8 * line)
    plain = size != 64 or rows % 64 != 0
    if plain:
        parts = grad.reshape(rows, line, 2, 2, 2, size)
        grad = parts.transpose(0, 3, 1, 4, 2, 5).reshape(rows, model)

    def whole(grad, x, base, gain):
        x = x.astype(F32)
        scale = lax.rsqrt(jnp.mean(x * x, axis=-1, keepdims=True) + EPS)
        scaled = gain * grad
        mean = jnp.mean(scaled * x, axis=-1, keepdims=True)
        out = base.astype(F32) + scale * scaled - x * (scale * scale * scale * mean)
        return out, jnp.sum(grad * x * scale, axis=0, keepdims=True)

    if plain:
        out, term = whole(grad if extra is None else grad + extra, x, base, gain)
        return (out.astype(BF16), term) if narrow else (out, out.astype(BF16), term)

    def kernel(*refs):
        grad_ref, refs = refs[0], refs[1:]
        extra_ref = None
        if extra is not None:
            extra_ref, refs = refs[0], refs[1:]
        x_ref, base_ref, gain_ref, refs = refs[0], refs[1], refs[2], refs[3:]
        held_ref, term_ref, refs = refs[0], refs[1], refs[2:]
        for (one, two), (low, high) in tile_order(line):
            got = swap_halves(grad_ref[:, columns(low)], grad_ref[:, columns(high)])
            for tile, part in zip((one, two), got):
                if extra_ref is not None:
                    part = part + extra_ref[:, columns(tile)]
                held_ref[:, columns(tile)] = part
        out, term = whole(held_ref[...], x_ref[...], base_ref[...], gain_ref[...])
        held_ref[...] = out
        for ref in refs:
            ref[...] = out.astype(BF16)

        @pl.when(pl.program_id(0) == 0)
        def _():
            term_ref[...] = term

        @pl.when(pl.program_id(0) > 0)
        def _():
            term_ref[...] += term

    arrays = [grad] + ([] if extra is None else [extra]) + [x, base, gain]
    outs = [(x.shape, F32), ((1, model), F32), (x.shape, BF16)]
    wide, term, low = rows_call(kernel, rows, outs, *arrays)
    return (low, term) if narrow else (wide, low, term)


def in_side_order(here, two):
    return jnp.where(here.side == 0, two, two[::-1])


def carry_states(here, states, decays, backward):
    states, decays = in_side_order(here, states), in_side_order(here, decays)
    other_states = here.over_core(states.astype(BF16)).astype(F32)
    other_decays = here.over_core(decays)
    first = here.core == 0
    state_at = [jnp.where(first, states, other_states), jnp.where(first, other_states, states)]
    decay_at = [jnp.where(first, decays, other_decays), jnp.where(first, other_decays, decays)]
    order = [(j, c) for j in range(2) for c in range(2)]
    if backward:
        order = order[::-1]
    parts = [(state_at[c][j], decay_at[c][j]) for j, c in order]
    total, through = parts[0]
    for state, decay in parts[1:]:
        total = decay * total + state
        through = through * decay
    half = total.shape[0] // 2
    mine = lax.dynamic_slice_in_dim(total, here.core * half, half, 0)
    row = jnp.pad(through[None, :], ((0, 15), (0, 0)))
    packed = jnp.concatenate([mine, row]).astype(BF16)
    entering = jnp.zeros_like(mine)
    for step in range(here.line_size - 1, 0, -1):
        came = here.along(packed, -step if backward else step).astype(F32)
        entering = came[half] * entering + came[:half]
    entering = pair(here.core, entering, here.over_core(entering)).reshape(total.shape)
    at = {}
    for (j, c), (state, decay) in zip(order, parts):
        at[j, c] = entering
        entering = decay * entering + state
    out = jnp.where(first, jnp.stack([at[0, 0], at[1, 0]]), jnp.stack([at[0, 1], at[1, 1]]))
    return in_side_order(here, out)


def recurrence_backward(
    leaving, out_grad, values, expanded, shrunk, ending, scores, states, running, logits, decay,
    count, flags,
):
    spans, length, width = running.shape
    value_width = values.shape[-1]
    segments = leaving.shape[0]
    per_seg = spans // segments

    def kernel(
        leaving_ref, o_ref, v_ref, exp_ref, shr_ref, end_ref, score_ref, state_ref, run_ref,
        logit_ref, decay_ref, count_ref, row_ref, flag_ref, grads_ref, logit_grad_ref, carry,
    ):
        @pl.when(pl.program_id(1) == 0)
        def _():
            carry[...] = leaving_ref[0]

        def nt(a, b):
            return lax.dot_general(a, b, (((1,), (1,)), ((), ())), preferred_element_type=F32)

        def tn(a, b):
            return lax.dot_general(a, b, (((0,), (0,)), ((), ())), preferred_element_type=F32)

        o, v = o_ref[0], v_ref[0]
        expanded, shrunk, ending = exp_ref[0], shr_ref[0], end_ref[0]
        state, score = state_ref[0], score_ref[0]
        counts, count_row = count_ref[0], row_ref[0]
        unfinished = counts == 0.0
        tail = counts == counts[length - 1 :]
        above = lax.broadcasted_iota(jnp.int32, (length, length), 0)
        below = lax.broadcasted_iota(jnp.int32, (length, length), 1)
        mask = (counts == count_row) & (above >= below)
        later = carry[...]
        later_low = later.astype(BF16)

        score_grad = jnp.where(mask, nt(o, v), 0.0).astype(BF16)
        expanded_grad = dot(score_grad, shrunk) + jnp.where(unfinished, dot(o, state), 0.0)
        shrunk_grad = tn(score_grad, expanded)
        ending_grad = dot(v, later_low)
        value_grad = tn(score, o) + nt(ending, later_low)
        running = run_ref[0]
        to_end = jnp.where(tail, jnp.exp(running[length - 1 :] - running), 0.0)
        query_grad = expanded_grad * jnp.exp(running) * HK ** (-0.5)
        key_grad = shrunk_grad * jnp.exp(-running) + ending_grad * to_end
        grads_ref[:, :width] = query_grad.astype(BF16)
        grads_ref[:, width : 2 * width] = key_grad.astype(BF16)
        grads_ref[:, 2 * width :] = value_grad.astype(BF16)

        from_here = expanded.astype(F32) * expanded_grad - shrunk.astype(F32) * shrunk_grad
        from_past = ending.astype(F32) * ending_grad
        decay = decay_ref[0]
        carried = decay * jnp.sum(state.astype(F32) * later, axis=0, keepdims=True)
        upper = (below >= above).astype(F32)
        lower = (below < above).astype(F32)
        decay_grad = carried
        for triangle, terms in ((upper, from_here), (lower, from_past)):
            decay_grad = decay_grad + jnp.dot(
                triangle, terms, precision=lax.Precision.HIGHEST, preferred_element_type=F32
            )
        decay_grad = decay_grad * (1.0 - flag_ref[0])
        logits = logit_ref[0]
        logit_grad_ref[...] = (decay_grad * jax.nn.sigmoid(-logits) / GATE_SCALE).astype(BF16)

        reach = jnp.where(unfinished, expanded.astype(F32), 0.0).astype(BF16)
        carry[...] = decay * later + tn(o, reach)

    def at(j, c):
        return j * per_seg + per_seg - 1 - c

    def spec(array):
        return pl.BlockSpec((1,) + array.shape[1:], lambda j, c: (at(j, c), 0, 0))

    arrays = [
        out_grad, values, expanded, shrunk, ending, scores, states, running, logits,
        decay.reshape(spans, 1, width), count.reshape(spans, length, 1),
        count.reshape(spans, 1, length), flags.reshape(spans, length, 1),
    ]
    moved = sum(a.size * a.dtype.itemsize for a in arrays)
    tall = 2 * width + value_width
    return pl.pallas_call(
        kernel,
        grid=(segments, per_seg),
        in_specs=[pl.BlockSpec((1, value_width, width), lambda j, c: (j, 0, 0))]
        + [spec(a) for a in arrays],
        out_specs=[
            pl.BlockSpec((length, tall), lambda j, c: (at(j, c), 0)),
            pl.BlockSpec((length, width), lambda j, c: (at(j, c), 0)),
        ],
        out_shape=[
            jax.ShapeDtypeStruct((spans * length, tall), BF16),
            jax.ShapeDtypeStruct((spans * length, width), BF16),
        ],
        scratch_shapes=[pltpu.VMEM((value_width, width), F32)],
        compiler_params=pltpu.CompilerParams(vmem_limit_bytes=56 * 2**20),
        cost_estimate=pl.CostEstimate(
            flops=10 * spans * length * width * value_width,
            bytes_accessed=moved,
            transcendentals=4 * running.size,
        ),
    )(leaving, *arrays)


def on_device(
    tokens,
    attn_gain,
    w_query,
    w_key,
    w_value,
    w_down_rank,
    w_up_rank,
    gate_bias,
    w_outgate,
    head_gain,
    w_output,
    ffn_gain,
    w_gate,
    w_up,
    w_down,
    doc_starts,
    cotangent,
):
    here = Place()
    line = here.line_size
    tok, model = tokens.shape
    rows_d = w_query.shape[0]
    rows_f = w_down.shape[0]
    rank = w_up_rank.shape[0]
    cols_k = w_up_rank.shape[1]
    group = 4 * tok
    spans = group // SPAN
    per_seg = spans // 2
    me = 2 * here.seq + here.side

    small = jnp.concatenate(
        [
            attn_gain,
            ffn_gain,
            head_gain,
            gate_bias,
            w_up_rank.reshape(-1),
            w_down_rank.reshape(-1),
        ]
    )
    small_size = small.shape[0]
    small_rows = 8 * -(-small_size // (8 * model))
    small = jnp.pad(small, (0, small_rows * model - small_size)).reshape(small_rows, model)
    out_lines = gather_line(here, jnp.concatenate([here.swap_top(w_output), small]))
    out_lines = out_lines.reshape(line, 2, rows_d + small_rows, model)
    small_line = out_lines[:, :, rows_d:].reshape(line, 2, -1)[:, :, :small_size]
    w_out = out_lines[:, :, :rows_d].reshape(2, line // 2, 2 * rows_d, model)
    w_out = w_out.transpose(1, 0, 2, 3).reshape(HV, model)

    def heads_first(w, width):
        return w.reshape(rows_d, HEADS, width).transpose(1, 0, 2)

    def hidden_first(w):
        return (
            w.reshape(rows_d, 2, line, 2, 2, rows_f)
            .transpose(1, 3, 0, 2, 4, 5)
            .reshape(4, rows_d, -1)
        )

    quarter = 2 * line * rows_f
    mixer_cols = jnp.concatenate(
        [
            heads_first(w_query, HK),
            heads_first(w_key, HK),
            heads_first(w_value, HV),
            heads_first(w_outgate, HV),
        ],
        axis=2,
    )
    *mixer_quarters, tokens_in, w_gate, w_up = phase(
        *send_quarters(here, mixer_cols), to_gathered(tokens, line), w_gate, w_up
    )
    mixer_piece = join_quarters(here, *mixer_quarters).reshape(4 * rows_d, -1)
    w_mixer = gather_line(here, mixer_piece)
    other_docs = here.over_side(doc_starts)
    top_pair, low_pair, small_line, gate_cols, other_docs, w_up = phase(
        *near_halves(here, tokens_in), small_line, hidden_first(w_gate), other_docs, w_up
    )
    small_all = gather_small_plane(here, small_line)
    small_all, top_pair, low_pair, up_cols = phase(
        small_all, top_pair, low_pair, hidden_first(w_up)
    )
    ffn_cols = jnp.concatenate([gate_cols, up_cols], axis=2)
    top_far, low_far, ffn_cols, top_pair, low_pair = phase(
        *far_halves(here, top_pair, low_pair), ffn_cols, top_pair, low_pair
    )
    ffn_quarters = send_quarters(here, ffn_cols)
    wide_in = in_stream(here, top_pair, low_pair, top_far, low_far).astype(F32)
    cuts = []
    at = 0
    for size in (rows_d, rows_d, head_gain.shape[0], cols_k, rank * cols_k, rows_d * rank):
        cuts.append(small_all[:, at : at + size])
        at += size
    devices = small_all.shape[0]
    full_attn_gain = cuts[0].reshape(model).astype(F32)
    full_ffn_gain = cuts[1].reshape(model).astype(F32)
    full_head_gain = cuts[2].reshape(HV).astype(F32)
    full_bias = cuts[3].reshape(HEADS * HK)
    full_up_rank = cuts[4].reshape(devices, rank, cols_k).transpose(1, 0, 2).reshape(rank, -1)
    full_down_rank = cuts[5].reshape(model, rank)
    my_bias = lax.dynamic_slice_in_dim(full_bias, me * HK, HK, 0).astype(F32)
    my_up_rank = lax.dynamic_slice_in_dim(full_up_rank, me * HK, HK, 1)
    down_rank_rows = (
        full_down_rank.reshape(2, line, 2, 2, rows_d, rank)
        .transpose(1, 3, 0, 2, 4, 5)
        .reshape(model, rank)
    )

    wide_scale = lax.rsqrt(jnp.mean(wide_in * wide_in, axis=-1, keepdims=True) + EPS)
    x_in = (wide_in * wide_scale * to_gathered(full_attn_gain[None], line)).astype(BF16)
    rank_low = dot(x_in, down_rank_rows).astype(BF16)
    *ffn_quarters, x_in, rank_low, cotangent, w_down = phase(
        *ffn_quarters, x_in, rank_low, cotangent, w_down
    )
    ffn_piece = join_quarters(here, *ffn_quarters).reshape(4 * rows_d, -1)
    w_ffn = gather_line(here, ffn_piece)
    w_dn = gather_line(here, after(w_down, ffn_piece))
    cot_parts = here.over_side(cotangent), here.over_seq(cotangent), here.over_both(cotangent)

    inputs = tokens.astype(F32)
    scale_in = lax.rsqrt(jnp.mean(inputs * inputs, axis=-1, keepdims=True) + EPS)
    normed_in = (inputs * scale_in * full_attn_gain).astype(BF16)
    docs = jnp.stack([doc_starts, other_docs])
    flags = (jnp.arange(tok, dtype=jnp.int32) == docs[:, :, None]).astype(F32)
    flags = flags.reshape(spans, SPAN)

    projected = dot(x_in, w_mixer)
    queries = projected[:, :HK].astype(BF16)
    keys_in = projected[:, HK : 2 * HK].astype(BF16)
    values = projected[:, 2 * HK : 2 * HK + HV].astype(BF16)
    outgate = projected[:, 2 * HK + HV :]
    logits = (dot(rank_low, my_up_rank) + my_bias).astype(BF16).astype(F32)

    decays = (jax.nn.log_sigmoid(logits) / GATE_SCALE).reshape(spans, SPAN, HK)
    causal = jnp.tril(jnp.ones((SPAN, SPAN), F32))
    running = jnp.einsum("ts,nsk->ntk", causal, decays, precision=lax.Precision.HIGHEST)
    count = jnp.einsum("ts,ns->nt", causal, flags, precision=lax.Precision.HIGHEST)
    closing = running[:, -1, :]
    unfinished = (count == 0.0)[:, :, None]
    tail = (count == count[:, -1:])[:, :, None]
    unbroken = count[:, -1:] == 0.0
    mask = (count[:, :, None] == count[:, None, :]) & (causal > 0)[None]
    q_s = queries.reshape(spans, SPAN, HK).astype(F32) * HK ** (-0.5)
    k_s = keys_in.reshape(spans, SPAN, HK).astype(F32)
    v_s = values.reshape(spans, SPAN, HV)
    grow = jnp.exp(running)
    shrink = jnp.exp(-running)
    to_end = jnp.where(tail, jnp.exp(closing[:, None, :] - running), 0.0)
    expanded = q_s * grow
    shrunk = k_s * shrink
    ending = k_s * to_end
    expanded_low = expanded.astype(BF16)
    shrunk_low = shrunk.astype(BF16)
    ending_low = ending.astype(BF16)
    reach_low = jnp.where(unfinished, expanded, 0.0).astype(BF16)
    exact = lax.Precision.HIGHEST
    wide_scores = jnp.einsum("ntk,nsk->nts", expanded, shrunk, precision=exact)
    wide_scores = jnp.where(mask, wide_scores, 0.0)
    scores = wide_scores.astype(BF16)
    span_decay = jnp.where(unbroken, jnp.exp(closing), 0.0).reshape(2, per_seg, HK)
    updates = ein("ntv,ntk->nvk", v_s, ending_low).reshape(2, per_seg, HV, HK)

    before = [jnp.ones((2, HK), F32)]
    for c in range(per_seg):
        before.append(before[-1] * span_decay[:, c])
    through = before[-1]
    before = jnp.stack(before[:-1], axis=1)
    rest = [jnp.ones((2, HK), F32)]
    for c in range(per_seg - 1, 0, -1):
        rest.append(rest[-1] * span_decay[:, c])
    rest = jnp.stack(rest[::-1], axis=1)
    seg_ending = (ending.reshape(2, per_seg, SPAN, HK) * rest[:, :, None, :]).astype(BF16)
    seg_ending = seg_ending.reshape(2, per_seg * SPAN, HK)
    seg_values = values.reshape(2, per_seg * SPAN, HV)
    seg_end = ein("jtv,jtk->jvk", seg_values, seg_ending)
    *cot_parts, seg_end = phase(*cot_parts, seg_end)
    cot = in_loose(cotangent, *cot_parts)
    entering = carry_states(here, seg_end, through, False)
    states = [entering]
    for c in range(per_seg - 1):
        states.append(span_decay[:, c, None, :] * states[-1] + updates[:, c])
    states_low = jnp.stack([s.astype(BF16) for s in states], axis=1).reshape(spans, HV, HK)
    inside = jnp.einsum("nts,nsv->ntv", wide_scores, v_s.astype(F32), precision=exact)
    raw = inside + ein("ntk,nvk->ntv", reach_low, states_low)
    mixed = raw.reshape(group, HV).astype(BF16).astype(F32)

    head_scale = lax.rsqrt(jnp.mean(mixed * mixed, axis=-1, keepdims=True) + EPS)
    normed_mix = mixed * head_scale * full_head_gain
    outgate_sig = jax.nn.sigmoid(outgate)
    gate_act = outgate * outgate_sig
    gated = (normed_mix * gate_act).astype(BF16)
    branch_parts = near_sums(here, *stream_parts(here, dot(gated, w_out).astype(BF16)))
    branch_out = far_sums(here, *branch_parts)
    resid, normed_mid = norm_forward(tokens, branch_out, full_ffn_gain[None], line)
    x_mid = gather_loose(here, normed_mid)
    gate_up = dot(x_mid, w_ffn)
    gate_pre, up_pre = gate_up[:, :quarter], gate_up[:, quarter:]
    gate_sig = jax.nn.sigmoid(gate_pre)
    silu_gate = gate_pre * gate_sig
    hidden = (silu_gate * up_pre).astype(BF16)

    down_part = dot_rows(hidden, cot).astype(BF16)
    down_term = scatter_line(here, down_part)
    hidden_grad = dot_cols(after(cot, down_part), w_dn)
    gate_grad = (hidden_grad * up_pre * (gate_sig * (1.0 + gate_pre * (1.0 - gate_sig)))).astype(
        BF16
    )
    up_grad = (hidden_grad * silu_gate).astype(BF16)
    gate_up_grad = jnp.concatenate([gate_grad, up_grad], axis=1)
    rows_by_step = gate_up_grad.reshape(2, 2, 2, tok // 2, 2 * quarter)

    def mid_of(rows):
        return dot_cols(rows.reshape(2 * tok, -1), w_ffn).astype(BF16).reshape(2, 2, -1, model)

    to_send = mid_of(rows_by_step[:, :, 1])
    to_keep = mid_of(after(rows_by_step[:, :, 0], to_send))
    mid_parts = (to_keep[0], here.over_side(to_send[0]), to_keep[1], here.over_seq(to_send[1]))
    ffn_part = dot_rows(x_mid, gate_up_grad).astype(BF16)
    *mid_parts, ffn_part = phase(*mid_parts, ffn_part)
    mid_grad, down_term, ffn_part, hidden = phase(
        far_sums(here, *mid_parts), down_term, ffn_part, hidden
    )
    ffn_term = scatter_line(here, ffn_part)
    resid_grad, branch, ffn_gain_term = norm_backward(
        mid_grad, None, resid, cotangent, full_ffn_gain[None], line, False
    )
    near = near_halves(here, branch)
    *near, hidden = phase(*near, hidden)
    down_out = dot(hidden, w_dn).astype(BF16)
    *far, down_out = phase(*far_halves(here, *near), down_out)
    branch = in_stream(here, *near, *far)

    gated_grad = dot_cols(branch, w_out)
    outgate_grad = (
        gated_grad * normed_mix * outgate_sig * (1.0 + outgate * (1.0 - outgate_sig))
    ).astype(BF16)
    normed_grad = gated_grad * gate_act
    head_gain_term = jnp.sum(normed_grad * mixed * head_scale, axis=0)
    scaled_head = full_head_gain * normed_grad
    mixed_grad = (
        head_scale * scaled_head
        - mixed * head_scale**3 * jnp.mean(scaled_head * mixed, axis=-1, keepdims=True)
    ).astype(BF16)
    seg_reach = jnp.where(unfinished, expanded, 0.0).reshape(2, per_seg, SPAN, HK)
    seg_reach = (seg_reach * before[:, :, None, :]).astype(BF16)
    seg_reach = seg_reach.reshape(2, per_seg * SPAN, HK)
    start_grad = ein("jtv,jtk->jvk", mixed_grad.reshape(2, per_seg * SPAN, HV), seg_reach)
    leaving = carry_states(here, start_grad, through, True)
    out_term = dot_rows(gated, branch).astype(BF16)
    out_term = out_term.reshape(line // 2, 2, 2 * rows_d, model).transpose(1, 0, 2, 3)
    out_part = out_term.reshape(HV, model)
    leaving, out_part, down_out = phase(leaving, out_part, down_out)
    down_parts = near_sums(here, *loose_parts(down_out))
    out_term = scatter_line(here, after(out_part, ffn_term))

    mixer_grads, logit_grad = recurrence_backward(
        leaving,
        mixed_grad.reshape(spans, SPAN, HV),
        v_s,
        expanded_low,
        shrunk_low,
        ending_low,
        scores,
        states_low,
        running,
        logits.reshape(spans, SPAN, HK),
        span_decay,
        count,
        flags,
    )
    grads = jnp.concatenate([mixer_grads, outgate_grad], axis=1)
    in_part = dot_cols(grads, w_mixer).astype(BF16)
    attn_gain_here = jnp.sum(in_part.astype(F32) * (wide_in * wide_scale), axis=0)
    ffn_back = send_quarters(here, ffn_term.reshape(4, rows_d, 2 * quarter))
    in_part, out_term, down_top, down_top_in, down_low, down_low_in, *ffn_back = phase(
        in_part, out_term, *down_parts, *ffn_back
    )
    down_parts = down_top, down_top_in, down_low, down_low_in
    layer_output = (resid + far_sums(here, *down_parts)).astype(BF16)

    bias_term = jnp.sum(logit_grad.astype(F32), axis=0)
    up_rank_term = dot_rows(rank_low, logit_grad)
    rank_part = dot_cols(logit_grad, my_up_rank)
    other_side = here.over_side(rank_part[2 * tok :])
    rank_part = rank_part[: 2 * tok] + other_side
    rank_part = rank_part + here.over_seq(rank_part)
    rank_grad = lax.dynamic_slice_in_dim(rank_part, here.seq * tok, tok, 0).astype(BF16)
    down_rank_term = dot_rows(normed_in, rank_grad)
    rank_in_grad = dot_cols(rank_grad, full_down_rank)
    attn_gain_term = jnp.sum(rank_in_grad * (inputs * scale_in), axis=0)

    zero_bias = jnp.zeros((HEADS * HK,), F32)
    zero_up = jnp.zeros((rank, HEADS * HK), F32)
    bias_all = lax.dynamic_update_slice_in_dim(zero_bias, bias_term, me * HK, 0)
    up_all = lax.dynamic_update_slice_in_dim(zero_up, up_rank_term, me * HK, 1)
    small_terms = jnp.concatenate(
        [
            attn_gain_term.reshape(devices, -1)
            + attn_gain_here.reshape(line, 2, 2, 2, rows_d)
            .transpose(2, 0, 3, 1, 4)
            .reshape(devices, -1),
            ffn_gain_term.reshape(devices, -1),
            head_gain_term.reshape(devices, -1),
            bias_all.reshape(devices, -1),
            up_all.reshape(rank, devices, cols_k).transpose(1, 0, 2).reshape(devices, -1),
            down_rank_term.reshape(devices, -1),
        ],
        axis=1,
    )
    small_part = scatter_small_plane(here, small_terms)
    in_parts = near_sums(here, *stream_parts(here, after(in_part, small_part)))
    small_cols = 128 * -(-small_size // (512 * rows_d))
    small_part = jnp.pad(
        small_part.reshape(2 * line, small_size),
        ((0, 0), (0, 4 * rows_d * small_cols - small_size)),
    ).reshape(-1, small_cols)
    wide_grads = jnp.pad(grads, ((0, 0), (0, small_cols)))
    mixer_part = dot_rows(x_in, wide_grads).astype(BF16)
    mixer_part = lax.dynamic_update_slice(mixer_part, small_part.astype(BF16), (0, grads.shape[1]))
    mixer_part, out_term = phase(mixer_part, out_term)
    mixer_term = scatter_line(here, mixer_part)
    *in_parts, layer_output = phase(*in_parts, layer_output)
    in_grad = far_sums(here, *in_parts)

    input_grad, _ = norm_backward(
        in_grad,
        rank_in_grad,
        tokens,
        resid_grad,
        full_attn_gain[None],
        line,
        True,
    )

    down_grad = down_term.astype(F32)
    out_grad = here.swap_top(out_term).astype(F32)
    ffn_back = join_quarters(here, *ffn_back).astype(F32)

    def hidden_last(g):
        return (
            g.reshape(2, 2, rows_d, line, 2, rows_f)
            .transpose(2, 0, 3, 1, 4, 5)
            .reshape(rows_d, 4 * quarter)
        )

    gate_out = hidden_last(ffn_back[:, :, :quarter])
    up_out = hidden_last(ffn_back[:, :, quarter:])
    small_sum = mixer_term[:, 2 * HK + 2 * HV :].reshape(-1).astype(F32)
    mixer_term = after(
        mixer_term[:, : 2 * HK + 2 * HV], gate_out, up_out, out_grad, down_grad
    )
    mixer_back = send_quarters(here, mixer_term.reshape(4, rows_d, -1))
    mixer_back = join_quarters(here, *mixer_back).astype(F32)

    def heads_last(g):
        return g.transpose(1, 0, 2).reshape(rows_d, -1)

    query_out = heads_last(mixer_back[:, :, :HK])
    key_out = heads_last(mixer_back[:, :, HK : 2 * HK])
    value_out = heads_last(mixer_back[:, :, 2 * HK : 2 * HK + HV])
    outgate_out = heads_last(mixer_back[:, :, 2 * HK + HV :])
    small_sum = after(small_sum, query_out, key_out, value_out, outgate_out)
    pieces = []
    at = 0
    for size in (rows_d, rows_d, head_gain.shape[0], cols_k, rank * cols_k, rows_d * rank):
        pieces.append(small_sum[at : at + size])
        at += size
    return (
        layer_output,
        input_grad,
        pieces[0],
        query_out,
        key_out,
        value_out,
        pieces[5].reshape(rows_d, rank),
        pieces[4].reshape(rank, cols_k),
        pieces[3],
        outgate_out,
        pieces[2],
        out_grad,
        pieces[1],
        gate_out,
        up_out,
        down_grad,
    )


def solution(mesh):
    rows = P(BOTH, None)
    vector = P(BOTH)
    by_tokens = P(("fsdp", "seq"), None)
    by_cols = P(None, BOTH)
    in_specs = (
        by_tokens,
        vector,
        rows,
        rows,
        rows,
        rows,
        by_cols,
        vector,
        rows,
        vector,
        rows,
        vector,
        rows,
        rows,
        rows,
        P("fsdp"),
        by_tokens,
    )
    out_specs = (
        by_tokens,
        by_tokens,
        vector,
        rows,
        rows,
        rows,
        rows,
        by_cols,
        vector,
        rows,
        vector,
        rows,
        vector,
        rows,
        rows,
        rows,
    )
    return jax.shard_map(
        on_device, mesh=mesh, in_specs=in_specs, out_specs=out_specs, check_vma=False
    )
```
